32 devices in a mesh: seq: 8 (over z, x), tp: 4 (over y, core).
Axes of the slice: x: 2, y: 2, z: 4, core: 2. Of those that a mesh axis runs over, the one named last changes fastest.
Arguments:
- residual: bfloat16 [1536, 8192], P('seq', 'tp'), may hold values from -6 to 6
- attention: bfloat16 [384, 8192], P('seq'), may hold values from -6 to 6
- quantized_codes: int32 [8192, 8192], P('seq', 'tp'), may hold values from 0 to 15
- absmax: float32 [8192, 128], P('seq', 'tp'), may hold values from 0.005 to 0.05
- adapter_down: bfloat16 [8192, 64], P('seq'), may hold values from -0.0625 to 0.0625
- adapter_up: bfloat16 [64, 8192], P(None, 'tp'), may hold values from -0.75 to 0.75
- routed_slot_gate: float32 [384], P('seq'), may hold values from 0.2 to 1
- selected: int32 [384], P('seq'), may hold values from 0 to 191, as said below
- counts: int32 [8], P('seq'), may hold values from 1 to 48, 192 in all
- cotangent: bfloat16 [1536, 8192], P('seq', 'tp'), may hold values from -0.59765625 to 0.59765625
Outputs:
- outgoing_residual: bfloat16 [1536, 8192], P('seq', 'tp')
- attention_output_grad: bfloat16 [384, 8192], P(None, 'seq')
- adapter_down_gradient: float32 [8192, 64], P('seq')
- adapter_up_gradient: float32 [64, 8192], P(None, 'tp')
- router_gate_gradient: float32 [384], P('seq')
The draws below stay inside these ranges and needn't reach their ends.
Inputs may be any that keep to these rules, and one draw needn't show every extreme that they name: `counts`: every shard has at least one live slot, all shards together have 192, and some shard has all 48 slots live. `selected`: within each shard's 48 slots the entries are distinct token positions of that shard; only the first counts entries of a shard are live.
All inputs are finite; a program needn't handle non-finite values.
Results may differ from the reference program's by a relative error of at most 0.0058.
Values may be sent and summed in bfloat16 or wider, within the bound.
No kernel may reach another device: no remote copies, remote signals or barrier semaphores. Data moves between devices by JAX's collectives and lax.ppermute only.
A program may use at most 128 MiB of HBM per device.

```python
import math
import jax
import jax.numpy as jnp
import numpy as np
from jax import lax

MODEL_WIDTH = 8192
ADAPTER_RANK = 64
QBLOCK = 64
TOK_DEV = 192
HEAD_WIDTH_TOTAL = 8192
CAP = 48
TOKENS = 1536
SELECTED = 192
SLOTS = 384
N_SEQ = 8


def draw_selected(key, part):
    shard_keys = jax.random.split(key, TOKENS // TOK_DEV)

    def one_shard(shard_key):
        return jax.random.permutation(shard_key, TOK_DEV)[:CAP]
    return jax.vmap(one_shard)(shard_keys).reshape(-1).astype(jnp.int32)


def with_ends(array, rng, least, largest):
    longest = array.shape.index(max(array.shape))
    spots = []
    for shift in (0, 1):
        where = [jax.random.randint(jax.random.fold_in(rng, axis), (), 0, length) for axis, length in enumerate(array.shape)]
        where[longest] = (where[longest] + shift) % array.shape[longest]
        spots.append(tuple(where))
    return array.at[spots[0]].set(least).at[spots[1]].set(largest)


def levels(own_key, dims, pieces, smallest, largest):
    loudness, own = 1.0, jax.random.fold_in(own_key, 6)
    for dim, parts in pieces:
        heights = jnp.exp(jax.random.uniform(jax.random.fold_in(own, dim), (parts,), jnp.float32, smallest / len(pieces), largest / len(pieces)))
        loudness = loudness * jnp.repeat(heights, dims[dim] // parts).reshape([-1 if axis == dim else 1 for axis in range(len(dims))])
    return loudness


def profile(count, total, reach, slope):
    weights = [(1 << 20) // math.isqrt(rank ** slope) + 1 for rank in range(2, count + 1)]
    surplus, given = total - reach - (count - 1), [1] * (count - 1)
    while surplus > 0:
        candidates = [i for i in range(count - 1) if given[i] < reach]
        whole, left = sum([weights[i] for i in candidates]), surplus
        for i in candidates:
            extra = min(reach - given[i], max(1, left * weights[i] // whole), surplus)
            given[i] = given[i] + extra
            surplus = surplus - extra
    return np.array([reach] + given)


def ragged_sizes(stream_key, amount, total, reach, slope):
    if amount == 2:
        one = jax.random.randint(stream_key, (), max(1, total - reach), min(reach, total - 1) + 1)
        return jnp.stack([one, total - one])
    sizes = jnp.asarray(profile(amount, total, reach, slope), jnp.int32)
    couples = (amount - 1) // 2
    donor, taker = sizes[1:1 + 2 * couples:2], sizes[2:2 + 2 * couples:2]
    room = jnp.minimum(donor - 1, reach - taker)
    shifted = jax.random.randint(jax.random.fold_in(stream_key, 1), (couples,), 0, 1 << 20) % (room + 1)
    sizes = sizes.at[1:1 + 2 * couples:2].set(donor - shifted).at[2:2 + 2 * couples:2].set(taker + shifted)
    return sizes[jax.random.permutation(jax.random.fold_in(stream_key, 2), amount)]


def centred(key, shape, scale, most, cuts=(), kind=jnp.bfloat16):
    drawn = jax.random.normal(key, shape, jnp.float32) * scale
    if len(cuts) > 0:
        drawn = levels(key, shape, cuts, -0.22, 0.18) * drawn
    return jnp.clip(drawn, min=-most, max=most).astype(kind)


def setup_inputs(seed: int = 0) -> dict:
    key_of = jax.random.split(jax.random.key(seed), 11)
    return {
        "residual": centred(key_of[0], (TOKENS, MODEL_WIDTH), 1.0, 6.0, ((0, 8), (1, 4))),
        "attention": centred(key_of[1], (SLOTS, HEAD_WIDTH_TOTAL), 1.0, 6.0, ((0, 8),)),
        "quantized_codes": with_ends(jax.random.randint(key_of[2], (HEAD_WIDTH_TOTAL, MODEL_WIDTH), 0, 16), jax.random.fold_in(key_of[2], 1), 0, 15).astype(jnp.int32),
        "absmax": jnp.clip(jnp.exp(math.log(0.05) - 2.3025851 * jax.random.uniform(key_of[3], (HEAD_WIDTH_TOTAL, MODEL_WIDTH // QBLOCK), jnp.float32) ** levels(key_of[3], (HEAD_WIDTH_TOTAL, MODEL_WIDTH // QBLOCK), ((0, 8), (1, 4)), -0.2, 0.2)), 0.005, 0.05),
        "adapter_down": centred(key_of[4], (HEAD_WIDTH_TOTAL, ADAPTER_RANK), HEAD_WIDTH_TOTAL ** -0.5, 0.0625, ((0, 8),)),
        "adapter_up": centred(key_of[5], (ADAPTER_RANK, MODEL_WIDTH), ADAPTER_RANK ** -0.5, 0.75, ((1, 4),)),
        "routed_slot_gate": jnp.clip(0.2 + 0.8 * jax.random.uniform(key_of[6], (SLOTS,), jnp.float32) ** levels(key_of[6], (SLOTS,), ((0, 8),), -0.2, 0.2), 0.2, 1.0),
        "selected": draw_selected(jax.random.fold_in(key_of[10], 71), 0),
        "counts": ragged_sizes(key_of[8], N_SEQ, SELECTED, CAP, 2).astype(jnp.int32),
        "cotangent": centred(key_of[9], (TOKENS, MODEL_WIDTH), 0.1, 0.59765625, ((0, 8), (1, 4))),
    }


LEVELS = (-1.0, -0.6961928009986877, -0.5250730514526367, -0.39491748809814453,
          -0.28444138169288635, -0.18477343022823334, -0.09105003625154495, 0.0,
          0.07958029955625534, 0.16093020141124725, 0.24611230194568634, 0.33791524171829224,
          0.44070982933044434, 0.5626170039176941, 0.7229568362236023, 1.0)
adapter_scale = 0.25


def precise_matmul(left, right):
    return jnp.dot(left, right, precision=lax.Precision.HIGHEST, preferred_element_type=jnp.float32)


def reference(residual, attention, quantized_codes, absmax, adapter_down, adapter_up, routed_slot_gate, selected, counts, cotangent):
    lookup = jnp.asarray(LEVELS, jnp.float32)
    scales = jnp.repeat(absmax, QBLOCK, axis=1)
    projection_weight = (lookup[quantized_codes] * scales).astype(jnp.bfloat16)
    adapter_product = jnp.dot(attention, adapter_down, preferred_element_type=jnp.float32)
    block_output = jnp.dot(attention, projection_weight, preferred_element_type=jnp.float32) + adapter_scale * precise_matmul(adapter_product, adapter_up.astype(jnp.float32))
    slot_ids = jnp.arange(SLOTS, dtype=jnp.int32)
    shard_ids = slot_ids // CAP
    live_slot = (slot_ids % CAP) < counts[shard_ids]
    token = (shard_ids * TOK_DEV + selected).astype(jnp.int32)
    target = jnp.where(live_slot, token, TOKENS).astype(jnp.int32)
    picked = residual[token].astype(jnp.float32)
    updated = (picked + routed_slot_gate[:, None] * block_output).astype(jnp.bfloat16)
    outgoing_residual = residual.at[target].set(updated, mode="drop")
    upstream = jnp.where(live_slot[:, None], cotangent[token].astype(jnp.float32), 0.0)
    router_gate_gradient = jnp.sum(upstream * block_output, axis=1)
    output_gradient = (routed_slot_gate[:, None] * upstream).astype(jnp.bfloat16)
    adapter_rank_gradient = (adapter_scale * jnp.dot(output_gradient, adapter_up.T, preferred_element_type=jnp.float32)).astype(jnp.bfloat16)
    attention_output_grad = (jnp.dot(output_gradient, projection_weight.T, preferred_element_type=jnp.float32)
                 + jnp.dot(adapter_rank_gradient, adapter_down.T, preferred_element_type=jnp.float32)).astype(jnp.bfloat16)
    adapter_down_gradient = jnp.dot(attention.T, adapter_rank_gradient, preferred_element_type=jnp.float32)
    adapter_up_gradient = adapter_scale * precise_matmul(adapter_product.T, output_gradient.astype(jnp.float32))
    return outgoing_residual, attention_output_grad, adapter_down_gradient, adapter_up_gradient, router_gate_gradient
```

```python
import jax
import jax.numpy as jnp
from jax import lax
from jax.experimental import pallas as pl
from jax.experimental.pallas import tpu as pltpu
from jax.sharding import PartitionSpec as P

LEVELS = (
    -1.0,
    -0.6961928009986877,
    -0.5250730514526367,
    -0.39491748809814453,
    -0.28444138169288635,
    -0.18477343022823334,
    -0.09105003625154495,
    0.0,
    0.07958029955625534,
    0.16093020141124725,
    0.24611230194568634,
    0.33791524171829224,
    0.44070982933044434,
    0.5626170039176941,
    0.7229568362236023,
    1.0,
)
adapter_scale = 0.25
BF, F32, I32 = jnp.bfloat16, jnp.float32, jnp.int32
VMEM_LIMIT = 48 * 2**20


def dot(a, b, ca=1, cb=0):
    return lax.dot_general(a, b, (((ca,), (cb,)), ((), ())), preferred_element_type=F32)


def split2(x):
    hi = x.astype(BF)
    return hi, (x - hi.astype(F32)).astype(BF)


def split3(x):
    hi = x.astype(BF)
    rest = x - hi.astype(F32)
    mid = rest.astype(BF)
    return hi, mid, (rest - mid.astype(F32)).astype(BF)


def call(kernel, outs, *args, flops=0, scratch=(), in_specs=None, name=None):
    nbytes = sum(a.size * a.dtype.itemsize for a in args) + sum(
        o.size * o.dtype.itemsize for o in outs
    )
    whole = pl.BlockSpec(memory_space=pltpu.VMEM)
    return pl.pallas_call(
        kernel,
        out_shape=tuple(outs),
        in_specs=in_specs or [whole] * len(args),
        out_specs=tuple([whole] * len(outs)),
        scratch_shapes=list(scratch),
        compiler_params=pltpu.CompilerParams(vmem_limit_bytes=VMEM_LIMIT),
        cost_estimate=pl.CostEstimate(flops=flops, bytes_accessed=nbytes, transcendentals=0),
        name=name,
    )(*args)


def shape(dims, dtype):
    return jax.ShapeDtypeStruct(tuple(dims), dtype)


def column(row):
    k = row.shape[1]
    eye = lax.broadcasted_iota(I32, (k, k), 0) == lax.broadcasted_iota(I32, (k, k), 1)
    return jnp.sum(jnp.where(eye, row, jnp.zeros_like(row)), axis=1, keepdims=True)


def row_of(col):
    k = col.shape[0]
    eye = lax.broadcasted_iota(I32, (k, k), 0) == lax.broadcasted_iota(I32, (k, k), 1)
    return jnp.sum(jnp.where(eye, col, jnp.zeros_like(col)), axis=0, keepdims=True)


def tree_levels(codes):
    values = list(LEVELS)
    for bit in range(4):
        odd = (codes & (1 << bit)) != 0
        values = [jnp.where(odd, values[2 * i + 1], values[2 * i]) for i in range(len(values) // 2)]
    return values[0]


def dequant_kernel(codes_ref, absmax_ref, table_ref, weight_ref):
    rows, cols = codes_ref.shape
    blocks = absmax_ref.shape[1]
    parts = jnp.concatenate(split3(absmax_ref[...]), axis=1)
    spread = lax.broadcasted_iota(I32, (3 * blocks, cols), 0) % blocks == lax.broadcasted_iota(
        I32, (3 * blocks, cols), 1
    ) // (cols // blocks)
    scales = dot(parts, jnp.where(spread, 1.0, 0.0).astype(BF))
    table = jnp.broadcast_to(table_ref[0:1, :], (rows, 128))
    for c in range(cols // 128):
        part = slice(c * 128, c * 128 + 128)
        codes = codes_ref[:, part]
        if c % 3:
            level = jnp.take_along_axis(table, codes, axis=1, mode="promise_in_bounds")
        else:
            level = tree_levels(codes)
        weight_ref[:, part] = (level * scales[:, part]).astype(BF)


def dequantize(codes, absmax, table, part, parts):
    rows, cols = codes.shape
    own = rows // parts
    block = min(128, own)
    steps = own // block
    return pl.pallas_call(
        dequant_kernel,
        grid=(steps,),
        out_shape=shape((own, cols), BF),
        in_specs=[
            pl.BlockSpec((block, cols), lambda i: (part * steps + i, 0)),
            pl.BlockSpec((block, absmax.shape[1]), lambda i: (part * steps + i, 0)),
            pl.BlockSpec((8, 128), lambda i: (0, 0)),
        ],
        out_specs=pl.BlockSpec((block, cols), lambda i: (i, 0)),
        compiler_params=pltpu.CompilerParams(vmem_limit_bytes=VMEM_LIMIT),
        cost_estimate=pl.CostEstimate(
            flops=own * cols * 100, bytes_accessed=own * cols * 6, transcendentals=0
        ),
        name="dequantize",
    )(codes, absmax, table)


def solution(mesh):
    n, tp = mesh.shape["seq"], mesh.shape["tp"]
    half = n // 2
    order = list(range(0, n, 2)) + list(range(n - 1, 0, -2))

    def ring(step):
        return [(order[i], order[(i + step) % n]) for i in range(n)]

    def flip(size, bit):
        return [(i, i ^ bit) for i in range(size)]

    def place(shard):
        return jnp.where(shard % 2 == 0, shard // 2, n - 1 - shard // 2)

    def shard_at(position):
        position = lax.rem(position + 2 * n, n)
        return jnp.where(position < half, 2 * position, 2 * (n - 1 - position) + 1)

    def body(
        residual,
        attention,
        quantized_codes,
        absmax,
        adapter_down,
        adapter_up,
        routed_slot_gate,
        selected,
        counts,
        cotangent,
    ):
        cap, all_heads = attention.shape
        tokens, cols = residual.shape
        heads = all_heads // n
        rank = adapter_up.shape[0]
        sub = heads // 2
        slots = n * cap
        side = 2 * rank
        gate_row = routed_slot_gate.reshape(1, cap)
        selected_row = selected.reshape(1, cap)
        table = jnp.asarray([list(LEVELS) * 8] * 8, F32)
        smem = pl.BlockSpec(memory_space=pltpu.SMEM)
        vmem = pl.BlockSpec(memory_space=pltpu.VMEM)

        def me():
            return lax.axis_index("seq"), lax.axis_index("tp") % 2

        def live_row(counts_ref):
            return lax.broadcasted_iota(I32, (1, cap), 1) < counts_ref[0]

        def pick(counts_ref, selected_ref):
            at = lax.broadcasted_iota(I32, (tokens, cap), 0) == selected_ref[...]
            return jnp.where(at & live_row(counts_ref), 1.0, 0.0).astype(BF)

        def prepare(counts_ref, selected_ref, gate_ref, attention_ref, cot_ref, send_ref, own_ref, grad_ref, up_ref):
            seq, core = me()
            for k in range(half):
                for ref, flipped in ((send_ref, 1), (own_ref, 0)):
                    at = (seq ^ (2 * k + flipped)) * heads + core * sub
                    ref[k] = attention_ref[:, pl.ds(pl.multiple_of(at, 128), sub)]
            upstream = dot(pick(counts_ref, selected_ref), cot_ref[...], 0, 0)
            up_ref[...] = upstream.astype(BF)
            grad_ref[...] = (column(gate_ref[...]) * upstream).astype(BF)

        send, own, grad, upstream = call(
            prepare,
            [shape((half, cap, sub), BF)] * 2 + [shape((cap, cols), BF)] * 2,
            counts, selected_row, gate_row, attention, cotangent,
            in_specs=[smem] + [vmem] * 4, name="prepare",
        )

        across = lax.ppermute(send, "seq", flip(n, 1))
        pairs = jnp.stack([own, across], axis=1)
        fetched = [pairs[0]] + [lax.ppermute(pairs[k], "seq", flip(n, 2 * k)) for k in range(1, half)]
        slots_own = jnp.concatenate(fetched).reshape(slots, sub)
        slots_other = lax.ppermute(slots_own, "tp", flip(tp, 1))

        gathered = {0: (grad,)}
        going, coming = grad, grad
        for step in range(1, half):
            going, coming = lax.ppermute(going, "seq", ring(1)), lax.ppermute(coming, "seq", ring(-1))
            gathered[n - step], gathered[step] = (going,), (coming,)
        mid = cap // 2
        gathered[half] = (
            lax.ppermute(going[:mid], "seq", ring(1)),
            lax.ppermute(coming[mid:], "seq", ring(-1)),
        )

        parts = 4
        weight = [dequantize(quantized_codes, absmax, table, i, parts) for i in range(parts)]
        per = heads // parts

        def forward(own_ref, other_ref, down_ref, up_ref, *refs):
            w_refs, (out_ref, low_ref) = refs[:parts], refs[parts:]
            seq, core = me()
            a, b = own_ref[...], other_ref[...]
            att = jnp.concatenate([jnp.where(core == 0, a, b), jnp.where(core == 0, b, a)], axis=1)
            low = dot(att, down_ref[...])
            thrice = jnp.concatenate(split3(adapter_scale * low), axis=1)
            low_pad = jnp.concatenate([low, jnp.zeros_like(low)], axis=1)
            for j in range(n):
                low_ref[seq ^ j] = low_pad[j * cap : (j + 1) * cap]
            spots = [lax.rem(place(seq ^ j) - place(seq) + n, n) for j in range(n)]
            tile = min(512, cols)
            for c in range(cols // tile):
                part = slice(c * tile, (c + 1) * tile)
                ups = up_ref[:, part]
                acc = dot(thrice, jnp.concatenate([ups] * 3, axis=0))
                for i in range(parts):
                    acc += dot(att[:, i * per : (i + 1) * per], w_refs[i][:, part])
                acc = acc.astype(BF)
                for j in range(n):
                    out_ref[spots[j], :, part] = acc[j * cap : (j + 1) * cap]

        partial, low = call(
            forward,
            [shape((n, cap, cols), BF), shape((n, cap, 2 * rank), F32)],
            slots_own, slots_other, adapter_down, adapter_up, *weight,
            flops=2 * slots * heads * cols, name="forward",
        )

        bit = 1
        while bit < n:
            low = low + lax.ppermute(low, "seq", flip(n, bit))
            bit *= 2

        def plus(a, b):
            return (a.astype(F32) + b.astype(F32)).astype(BF)

        going = lax.ppermute(partial[half, :mid], "seq", ring(1))
        coming = lax.ppermute(partial[half, mid:], "seq", ring(-1))
        for step in range(half - 1, 0, -1):
            here, there = partial[step], partial[n - step]
            if step == half - 1:
                here = jnp.concatenate([plus(here[:mid], going), here[mid:]])
                there = jnp.concatenate([there[:mid], plus(there[mid:], coming)])
            else:
                here, there = plus(here, going), plus(there, coming)
            going = lax.ppermute(here, "seq", ring(1))
            coming = lax.ppermute(there, "seq", ring(-1))

        def home(counts_ref, selected_ref, gate_ref, res_ref, own_ref, going_ref, coming_ref, up_ref, out_ref, gate_out_ref):
            chosen = pick(counts_ref, selected_ref)
            block = own_ref[...].astype(F32) + going_ref[...].astype(F32) + coming_ref[...].astype(F32)
            gate_out_ref[...] = row_of(jnp.sum(up_ref[...].astype(F32) * block, axis=1, keepdims=True))
            res = res_ref[...]
            picked = dot(chosen, res, 0, 0)
            updated = (picked + column(gate_ref[...]) * block).astype(BF)
            hit = jnp.sum(chosen.astype(F32), axis=1, keepdims=True) > 0
            out_ref[...] = jnp.where(hit, dot(chosen, updated), res.astype(F32)).astype(BF)

        outgoing_residual, gate_part = call(
            home,
            [shape((tokens, cols), BF), shape((1, cap), F32)],
            counts, selected_row, gate_row, residual, partial[0], going, coming, upstream,
            in_specs=[smem] + [vmem] * 7, name="home",
        )
        bit = 1
        while bit < tp:
            gate_part = gate_part + lax.ppermute(gate_part, "tp", flip(tp, bit))
            bit *= 2

        spots = [r for r in range(n) if r != half]
        some = slots // 2

        def backward(up_ref, *refs):
            w_refs, refs = refs[:parts], refs[parts:]
            first_ref, second_ref, refs = refs[0], refs[1], refs[2:]
            g_refs, (keep_ref, send_ref, all_ref, sums) = refs[: n - 1], refs[n - 1 :]
            seq, core = me()
            for r, ref in zip(spots, g_refs):
                all_ref[shard_at(place(seq) + r)] = ref[...]
            all_ref[shard_at(place(seq) + half)] = jnp.concatenate([first_ref[...], second_ref[...]])
            g = all_ref[...].reshape(slots, cols)
            for i in range(parts):
                sums[:, i * per : (i + 1) * per] = dot(g, w_refs[i][...], 1, 1)
            hi, lo = split2(adapter_scale * dot(g, up_ref[...], 1, 1))
            sums[:, heads:] = jnp.concatenate([hi, lo], axis=1).astype(F32)
            keep_ref[...] = sums[pl.ds(pl.multiple_of(core * some, 8), some), :]
            send_ref[...] = sums[pl.ds(pl.multiple_of((1 - core) * some, 8), some), :].astype(BF)

        wide = heads + side
        keep, send, grad_all = call(
            backward,
            [shape((some, wide), F32), shape((some, wide), BF), shape((n, cap, cols), BF)],
            adapter_up, *weight, *gathered[half], *[gathered[r][0] for r in spots],
            flops=2 * slots * heads * cols, scratch=[pltpu.VMEM((slots, wide), F32)], name="backward",
        )

        def ranks(a, b):
            return (a[:, heads : heads + rank].astype(F32) + b[:, heads : heads + rank].astype(F32)) + (
                a[:, heads + rank :].astype(F32) + b[:, heads + rank :].astype(F32)
            )

        def add(a_ref, b_ref, out_ref):
            a, b = a_ref[...], b_ref[...]
            out_ref[:, :heads] = (a[:, :heads].astype(F32) + b[:, :heads].astype(F32)).astype(BF)
            out_ref[:, heads:] = jnp.concatenate(split2(ranks(a, b)), axis=1)

        mine = call(add, [shape((some, wide), BF)], keep, lax.ppermute(send, "tp", flip(tp, 1)), name="add")[0]
        bit = 2
        while 2 * bit < tp:
            mine = call(add, [shape((some, wide), BF)], mine, lax.ppermute(mine, "tp", flip(tp, bit)), name="add")[0]
            bit *= 2

        def finish(a_ref, b_ref, down_ref, out_ref):
            a, b = a_ref[...], b_ref[...]
            rank_grad = ranks(a, b).astype(BF)
            tail = dot(rank_grad, down_ref[...], 1, 1)
            out_ref[:, :heads] = (a[:, :heads].astype(F32) + b[:, :heads].astype(F32) + tail).astype(BF)
            out_ref[:, heads:] = jnp.concatenate([rank_grad, jnp.zeros_like(rank_grad)], axis=1)

        done = call(
            finish, [shape((some, wide), BF)], mine, lax.ppermute(mine, "tp", flip(tp, bit)), adapter_down, name="finish"
        )[0]
        other_done = lax.ppermute(done, "tp", flip(tp, 1))

        def last(a_ref, b_ref, own_ref, other_ref, grad_ref, down_grad_ref, rank_ref):
            seq, core = me()
            for ref, at in ((a_ref, core), (b_ref, 1 - core)):
                grad_ref[pl.ds(pl.multiple_of(at * some, 16), some), :] = ref[:, :heads]
                for i in range(half):
                    rank_ref[at * half + i] = ref[i * cap : (i + 1) * cap, heads : heads + rank]
            rank_grad = jnp.concatenate([rank_ref[seq ^ j] for j in range(n)], axis=0)
            for ref, at in ((own_ref, core), (other_ref, 1 - core)):
                down_grad_ref[pl.ds(pl.multiple_of(at * sub, 8), sub), :] = dot(ref[...], rank_grad, 0, 0)

        attention_output_grad, adapter_down_gradient = call(
            last,
            [shape((slots, heads), BF), shape((heads, rank), F32)],
            done, other_done, slots_own, slots_other,
            scratch=[pltpu.VMEM((n, cap, rank), BF)], name="last",
        )

        def up_gradient(low_ref, g_ref, out_ref):
            low = low_ref[...].reshape(slots, 2 * rank)[:, :rank]
            thrice = dot(jnp.concatenate(split3(low), axis=1), g_ref[...].reshape(slots, cols), 0, 0)
            out_ref[...] = adapter_scale * (
                thrice[:rank] + thrice[rank : 2 * rank] + thrice[2 * rank :]
            )

        adapter_up_gradient = call(
            up_gradient, [shape((rank, cols), F32)], low, grad_all, flops=6 * slots * rank * cols, name="up_gradient"
        )[0]
        return (
            outgoing_residual,
            attention_output_grad,
            adapter_down_gradient,
            adapter_up_gradient,
            gate_part.reshape(cap),
        )

    return jax.shard_map(
        body,
        mesh=mesh,
        in_specs=(
            P("seq", "tp"),
            P("seq", None),
            P("seq", "tp"),
            P("seq", "tp"),
            P("seq", None),
            P(None, "tp"),
            P("seq"),
            P("seq"),
            P("seq"),
            P("seq", "tp"),
        ),
        out_specs=(P("seq", "tp"), P(None, "seq"), P("seq", None), P(None, "tp"), P("seq")),
        check_vma=False,
    )
```

```python
import functools

import jax
import jax.numpy as jnp
from jax import lax
from jax.experimental import pallas as pl
from jax.experimental.pallas import tpu as pltpu
from jax.sharding import PartitionSpec as P

LEVELS = (
    -1.0,
    -0.6961928009986877,
    -0.5250730514526367,
    -0.39491748809814453,
    -0.28444138169288635,
    -0.18477343022823334,
    -0.09105003625154495,
    0.0,
    0.07958029955625534,
    0.16093020141124725,
    0.24611230194568634,
    0.33791524171829224,
    0.44070982933044434,
    0.5626170039176941,
    0.7229568362236023,
    1.0,
)
adapter_scale = 0.25
BF, F32, I32 = jnp.bfloat16, jnp.float32, jnp.int32
VMEM_LIMIT = 16 * 2**20
DEAD = 2.0


def dot(a, b, ca=1, cb=0):
    return lax.dot_general(a, b, (((ca,), (cb,)), ((), ())), preferred_element_type=F32)


def split2(x):
    hi = x.astype(BF)
    return hi, (x - hi.astype(F32)).astype(BF)


def split3(x):
    hi = x.astype(BF)
    rest = x - hi.astype(F32)
    mid = rest.astype(BF)
    return hi, mid, (rest - mid.astype(F32)).astype(BF)


def call(kernel, outs, *args, flops=0, scratch=(), in_specs=None, name=None):
    nbytes = sum(a.size * a.dtype.itemsize for a in args) + sum(
        o.size * o.dtype.itemsize for o in outs
    )
    whole = pl.BlockSpec(memory_space=pltpu.VMEM)
    return pl.pallas_call(
        kernel,
        out_shape=tuple(outs),
        in_specs=in_specs or [whole] * len(args),
        out_specs=tuple([whole] * len(outs)),
        scratch_shapes=list(scratch),
        compiler_params=pltpu.CompilerParams(vmem_limit_bytes=VMEM_LIMIT),
        cost_estimate=pl.CostEstimate(flops=flops, bytes_accessed=nbytes, transcendentals=0),
        name=name,
    )(*args)


def shape(dims, dtype):
    return jax.ShapeDtypeStruct(tuple(dims), dtype)


def column(row):
    k = row.shape[1]
    eye = lax.broadcasted_iota(I32, (k, k), 0) == lax.broadcasted_iota(I32, (k, k), 1)
    return jnp.sum(jnp.where(eye, row, jnp.zeros_like(row)), axis=1, keepdims=True)


def row_of(col):
    k = col.shape[0]
    eye = lax.broadcasted_iota(I32, (k, k), 0) == lax.broadcasted_iota(I32, (k, k), 1)
    return jnp.sum(jnp.where(eye, col, jnp.zeros_like(col)), axis=0, keepdims=True)


def tree_levels(codes):
    values = list(LEVELS)
    for bit in range(4):
        odd = (codes & (1 << bit)) != 0
        values = [jnp.where(odd, values[2 * i + 1], values[2 * i]) for i in range(len(values) // 2)]
    return values[0]


def dequant_kernel(first, codes_hbm, absmax_ref, weight_ref, token_ref, codes, sems):
    chunks, block, cols = codes.shape
    blocks = absmax_ref.shape[1]
    per = cols // blocks

    def copy(i):
        rows = pl.ds(first + i * block, block)
        return pltpu.make_async_copy(codes_hbm.at[rows], codes.at[i], sems.at[i])

    for i in range(chunks):
        copy(i).start()
    token_ref[...] = jnp.zeros_like(token_ref)
    column_block = lax.broadcasted_iota(I32, (block, 128), 1) // per

    @pl.loop(0, chunks)
    def _(i):
        rows = pl.ds(pl.multiple_of(i * block, block), block)
        absmax = absmax_ref[pl.ds(pl.multiple_of(first + i * block, block), block), :]
        absmax = jnp.concatenate([absmax] * (128 // blocks), axis=1)
        copy(i).wait()
        for c in range(cols // 128):
            part = slice(c * 128, c * 128 + 128)
            scale = jnp.take_along_axis(absmax, column_block + c * (128 // per), axis=1, mode="promise_in_bounds")
            weight_ref[rows, part] = (tree_levels(codes[i, :, part]) * scale).astype(BF)


def in_hbm(array):
    return pltpu.with_memory_space_constraint(array, pltpu.HBM)


def solution(mesh):
    n, tp = mesh.shape["seq"], mesh.shape["tp"]
    half = n // 2
    order = list(range(0, n, 2)) + list(range(n - 1, 0, -2))

    def ring(step):
        return [(order[i], order[(i + step) % n]) for i in range(n)]

    def flip(size, bit):
        return [(i, i ^ bit) for i in range(size)]

    def place(shard):
        return jnp.where(shard % 2 == 0, shard // 2, n - 1 - shard // 2)

    def shard_at(position):
        position = lax.rem(position + 2 * n, n)
        return jnp.where(position < half, 2 * position, 2 * (n - 1 - position) + 1)

    def body(
        residual,
        attention,
        quantized_codes,
        absmax,
        adapter_down,
        adapter_up,
        routed_slot_gate,
        selected,
        counts,
        cotangent,
    ):
        cap, all_heads = attention.shape
        tokens, cols = residual.shape
        heads = all_heads // n
        rank = adapter_up.shape[0]
        sub = heads // 2
        slots = n * cap
        side = 2 * rank
        down_t = adapter_down.T
        gate_row = routed_slot_gate.reshape(1, cap)
        selected_row = selected.reshape(1, cap)
        hbm = pl.BlockSpec(memory_space=pltpu.HBM)
        smem = pl.BlockSpec(memory_space=pltpu.SMEM)
        vmem = pl.BlockSpec(memory_space=pltpu.VMEM)

        def me():
            return lax.axis_index("seq"), lax.axis_index("tp") % 2

        def live_row(counts_ref):
            return lax.broadcasted_iota(I32, (1, cap), 1) < counts_ref[0]

        def pick(counts_ref, selected_ref):
            at = lax.broadcasted_iota(I32, (tokens, cap), 0) == selected_ref[...]
            return jnp.where(at & live_row(counts_ref), 1.0, 0.0).astype(BF)

        some = slots // 4
        live_slots = slots // 2

        def prepare(counts_ref, selected_ref, gate_ref, attention_ref, cot_ref, send_ref, own_ref, grad_ref, up_ref, chosen, gates, cots, sems):
            seq, core = me()
            first = [
                pltpu.make_async_copy(selected_ref, chosen, sems.at[0]),
                pltpu.make_async_copy(gate_ref, gates, sems.at[1]),
                pltpu.make_async_copy(cot_ref, cots, sems.at[2]),
            ]
            later = []
            for k in range(half):
                for ref, flipped in ((send_ref, 1), (own_ref, 0)):
                    at = pl.multiple_of((seq ^ (2 * k + flipped)) * heads + core * sub, 128)
                    sem = sems.at[3 + 2 * k + flipped]
                    later.append(pltpu.make_async_copy(attention_ref.at[:, pl.ds(at, sub)], ref.at[k], sem))
            for copy in first + later:
                copy.start()
            for copy in first:
                copy.wait()
            upstream = dot(pick(counts_ref, chosen), cots[...], 0, 0)
            up_ref[...] = upstream.astype(BF)
            live = column(jnp.where(live_row(counts_ref), 1.0, 0.0)) > 0
            grad_ref[...] = jnp.where(live, column(gates[...]) * upstream, DEAD).astype(BF)
            for copy in later:
                copy.wait()

        send, own, grad, upstream = call(
            prepare,
            [shape((half, cap, sub), BF)] * 2 + [shape((cap, cols), BF)] * 2,
            counts, in_hbm(selected_row), in_hbm(gate_row), in_hbm(attention), in_hbm(cotangent),
            in_specs=[smem] + [hbm] * 4,
            scratch=[
                pltpu.VMEM((1, cap), I32),
                pltpu.VMEM((1, cap), F32),
                pltpu.VMEM((tokens, cols), BF),
                pltpu.SemaphoreType.DMA((3 + n,)),
            ],
            name="prepare",
        )

        across = lax.ppermute(send, "seq", flip(n, 1))
        going, coming = lax.ppermute(grad, "seq", ring(1)), lax.ppermute(grad, "seq", ring(-1))
        block = min(64, sub)

        def dequantize(part, absmax):
            return call(
                functools.partial(dequant_kernel, part * sub), [shape((sub, cols), BF), shape((8, 128), F32)],
                in_hbm(quantized_codes), absmax,
                in_specs=[hbm, vmem], flops=sub * cols * 100, name="dequantize",
                scratch=[
                    pltpu.VMEM((sub // block, block, cols), I32),
                    pltpu.SemaphoreType.DMA((sub // block,)),
                ],
            )

        weights, marks = zip(dequantize(0, absmax), dequantize(1, absmax))
        across, going, coming, mark = lax.optimization_barrier((across, going, coming, marks[0]))

        gathered = {0: (grad,)}

        def hop(step, going, coming):
            gathered[n - step], gathered[step] = (going,), (coming,)
            return lax.ppermute(going, "seq", ring(1)), lax.ppermute(coming, "seq", ring(-1))

        def pair(own_ref, across_ref, token_ref, *refs):
            for k, ref in enumerate(refs):
                ref[0] = own_ref[k]
                ref[1] = across_ref[k]

        def join(*refs):
            *refs, token_ref, out_ref = refs
            for k, ref in enumerate(refs):
                out_ref[2 * k * cap : 2 * (k + 1) * cap, :] = ref[...].reshape(2 * cap, sub)

        pairs = call(pair, [shape((2, cap, sub), BF)] * half, own, across, mark, name="pair")
        fetched = [pairs[0]] + [lax.ppermute(pairs[k], "seq", flip(n, 2 * k)) for k in range(1, half)]
        going, coming = hop(1, going, coming)
        fetched, going, coming, mark = lax.optimization_barrier((fetched, going, coming, marks[1]))
        slots_own = call(join, [shape((slots, sub), BF)], *fetched, mark, name="join")[0]
        slots_other = lax.ppermute(slots_own, "tp", flip(tp, 1))
        for step in range(2, half - 1):
            going, coming = hop(step, going, coming)
        mid = cap // 2

        def forward(own_ref, other_ref, down_ref, up_ref, w0_ref, w1_ref, out_ref, low_ref):
            seq, core = me()
            a, b = own_ref[...], other_ref[...]
            att = jnp.concatenate([jnp.where(core == 0, a, b), jnp.where(core == 0, b, a)], axis=1)
            low = dot(att, down_ref[...], 1, 1)
            thrice = jnp.concatenate(split3(adapter_scale * low), axis=1)
            for j in range(n):
                low_ref[seq ^ j] = low[j * cap : (j + 1) * cap]
            spots = [lax.rem(place(seq ^ j) - place(seq) + n, n) for j in range(n)]
            tile = min(512, cols)
            for c in range(cols // tile):
                part = slice(c * tile, (c + 1) * tile)
                ups = up_ref[:, part]
                acc = dot(thrice, jnp.concatenate([ups] * 3, axis=0))
                acc = acc + dot(att[:, :sub], w0_ref[:, part]) + dot(att[:, sub:], w1_ref[:, part])
                acc = acc.astype(BF)
                for j in range(n):
                    out_ref[spots[j], :, part] = acc[j * cap : (j + 1) * cap]

        partial, low = call(
            forward,
            [shape((n, cap, cols), BF), shape((n, cap, rank), F32)],
            slots_own, slots_other, down_t, adapter_up, *weights,
            flops=2 * slots * heads * cols, name="forward",
        )

        going, coming, partial = lax.optimization_barrier((going, coming, partial))
        gathered[n - half + 1], gathered[half - 1] = (going,), (coming,)
        gathered[half] = (
            lax.ppermute(going[:mid], "seq", ring(1)),
            lax.ppermute(coming[mid:], "seq", ring(-1)),
        )

        spots = [r for r in range(n) if r != half]

        def backward(low_ref, up_ref, w0_ref, w1_ref, first_ref, second_ref, *refs):
            g_refs, (keep_ref, send_ref, live_ref, where_ref, low_out_ref, every, sums) = refs[: n - 1], refs[n - 1 :]
            seq, core = me()
            for r, ref in zip(spots, g_refs):
                every[shard_at(place(seq) + r)] = ref[...]
            every[shard_at(place(seq) + half)] = jnp.concatenate([first_ref[...], second_ref[...]])
            passed = jnp.zeros((1, 1), F32)
            row = lax.broadcasted_iota(I32, (cap, live_slots), 0).astype(F32)
            col = lax.broadcasted_iota(I32, (cap, live_slots), 1).astype(F32)
            for j in range(n):
                alive = jnp.where(every[j][:, :1].astype(F32) < 0.5 * (1 + DEAD), 1.0, 0.0)
                at = jnp.where((row + passed == col) & (alive > 0), 1.0, 0.0)
                where_ref[j * cap : (j + 1) * cap, :] = at.astype(BF)
                passed = passed + jnp.sum(alive, axis=0, keepdims=True)
            g = dot(where_ref[...], every[...].reshape(slots, cols), 0, 0).astype(BF)
            live_ref[...] = g
            tile = min(256, sub)
            for i in range(sub // tile):
                for at, ref in ((0, w0_ref), (sub, w1_ref)):
                    sums[:, at + i * tile : at + (i + 1) * tile] = dot(g, ref[i * tile : (i + 1) * tile, :], 1, 1)
            low = dot(where_ref[...], jnp.concatenate(split3(low_ref[...].reshape(slots, rank)), axis=1), 0, 0)
            low = low[:, :rank] + low[:, rank : 2 * rank] + low[:, 2 * rank :]
            low_out_ref[...] = jnp.concatenate([low[:some], low[some:]], axis=1)
            hi, lo = split2(adapter_scale * dot(g, up_ref[...], 1, 1))
            sums[:, heads:] = jnp.concatenate([hi, lo], axis=1).astype(F32)
            keep_ref[...] = sums[pl.ds(pl.multiple_of(core * some, 8), some), :]
            send_ref[...] = sums[pl.ds(pl.multiple_of((1 - core) * some, 8), some), :].astype(BF)

        wide = heads + side

        def back(*farthest):
            return call(
                backward,
                [
                    shape((some, wide), F32),
                    shape((some, wide), BF),
                    shape((live_slots, cols), BF),
                    shape((slots, live_slots), BF),
                    shape((some, side), F32),
                ],
                low, adapter_up, *weights, *farthest, *[gathered[r][0] for r in spots],
                flops=2 * live_slots * heads * cols,
                scratch=[pltpu.VMEM((n, cap, cols), BF), pltpu.VMEM((live_slots, wide), F32)],
                name="backward",
            )

        def ranks(a, b):
            return (a[:, heads : heads + rank].astype(F32) + b[:, heads : heads + rank].astype(F32)) + (
                a[:, heads + rank :].astype(F32) + b[:, heads + rank :].astype(F32)
            )

        def add(a_ref, b_ref, out_ref):
            a, b = a_ref[...], b_ref[...]
            out_ref[:, :heads] = (a[:, :heads].astype(F32) + b[:, :heads].astype(F32)).astype(BF)
            out_ref[:, heads:] = jnp.concatenate(split2(ranks(a, b)), axis=1)

        def finish(a_ref, b_ref, down_ref, out_ref):
            a, b = a_ref[...], b_ref[...]
            rank_grad = ranks(a, b).astype(BF)
            tail = dot(rank_grad, down_ref[...])
            out_ref[:, :heads] = (a[:, :heads].astype(F32) + b[:, :heads].astype(F32) + tail).astype(BF)
            out_ref[:, heads:] = jnp.concatenate([rank_grad, jnp.zeros_like(rank_grad)], axis=1)

        def plus(a, b):
            return (a.astype(F32) + b.astype(F32)).astype(BF)

        def sum_heads(keep, send):
            recv = yield lax.ppermute(send, "tp", flip(tp, 1))
            mine = call(add, [shape((some, wide), BF)], keep, recv, name="add")[0]
            bit = 2
            while 2 * bit < tp:
                recv = yield lax.ppermute(mine, "tp", flip(tp, bit))
                mine = call(add, [shape((some, wide), BF)], mine, recv, name="add")[0]
                bit *= 2
            recv = yield lax.ppermute(mine, "tp", flip(tp, bit))
            done = call(finish, [shape((some, wide), BF)], mine, recv, down_t, name="finish")[0]
            other_done = yield lax.ppermute(done, "tp", flip(tp, 1))
            return done, other_done

        def sum_low(total):
            bit = 1
            while bit < n:
                recv = yield lax.ppermute(total, "seq", flip(n, bit))
                total = total + recv
                bit *= 2
            return total

        def drain(steps, value):
            try:
                while True:
                    value = steps.send(value)
            except StopIteration as stop:
                return stop.value

        here, there = partial[half, :mid], partial[half, mid:]
        going, coming = lax.ppermute(here, "seq", ring(1)), lax.ppermute(there, "seq", ring(-1))
        for step in range(half - 1, 0, -1):
            here, there = partial[step], partial[n - step]
            if step == half - 1:
                here = jnp.concatenate([plus(here[:mid], going), here[mid:]])
                there = jnp.concatenate([there[:mid], plus(there[mid:], coming)])
            else:
                here, there = plus(here, going), plus(there, coming)
            if step == half - 1:
                here, there, *farthest = lax.optimization_barrier((here, there, *gathered[half]))
                keep, send, grad_live, where_live, low_live = back(*farthest)
            elif step == half - 2:
                here, there, send = lax.optimization_barrier((here, there, send))
                head_steps, head_value = sum_heads(keep, send), None
            else:
                here, there, head_value, low_live = lax.optimization_barrier((here, there, head_value, low_live))
            going = lax.ppermute(here, "seq", ring(1))
            coming = lax.ppermute(there, "seq", ring(-1))
            if half - 4 < step < half - 1:
                head_value = head_steps.send(head_value)
        low_steps = sum_low(low_live)
        low_value = low_steps.send(None)
        going, coming, head_value, low_value = lax.optimization_barrier((going, coming, head_value, low_value))
        done, other_done = drain(head_steps, head_value)
        going, coming, done = lax.optimization_barrier((going, coming, done))
        low_sum = drain(low_steps, low_value)

        def home(counts_ref, selected_ref, gate_ref, res_ref, own_ref, going_ref, coming_ref, up_ref, out_ref, gate_out_ref):
            chosen = pick(counts_ref, selected_ref)
            block = own_ref[...].astype(F32) + going_ref[...].astype(F32) + coming_ref[...].astype(F32)
            gate_out_ref[...] = row_of(jnp.sum(up_ref[...].astype(F32) * block, axis=1, keepdims=True))
            res = res_ref[...]
            picked = dot(chosen, res, 0, 0)
            updated = (picked + column(gate_ref[...]) * block).astype(BF)
            hit = jnp.sum(chosen.astype(F32), axis=1, keepdims=True) > 0
            out_ref[...] = jnp.where(hit, dot(chosen, updated), res.astype(F32)).astype(BF)

        outgoing_residual, gate_part = call(
            home,
            [shape((tokens, cols), BF), shape((1, cap), F32)],
            counts, selected_row, gate_row, residual, partial[0], going, coming, upstream,
            in_specs=[smem] + [vmem] * 7, name="home",
        )
        bit = 1
        while bit < tp:
            gate_part = gate_part + lax.ppermute(gate_part, "tp", flip(tp, bit))
            bit *= 2

        def last(a_ref, b_ref, where_ref, own_ref, other_ref, grad_ref, down_grad_ref, live, rank_ref):
            seq, core = me()
            for ref, at in ((a_ref, core), (b_ref, 1 - core)):
                live[pl.ds(pl.multiple_of(at * some, 16), some), :] = ref[...]
            every = dot(where_ref[...], live[...]).astype(BF)
            grad_ref[...] = every[:, :heads]
            for j in range(n):
                rank_ref[j] = every[j * cap : (j + 1) * cap, heads:]
            rank_grad = jnp.concatenate([rank_ref[seq ^ j] for j in range(n)], axis=0)[:, :rank]
            for ref, at in ((own_ref, core), (other_ref, 1 - core)):
                down_grad_ref[:, pl.ds(pl.multiple_of(at * sub, 128), sub)] = dot(rank_grad, ref[...], 0, 0)

        attention_output_grad, down_gradient = call(
            last,
            [shape((slots, heads), BF), shape((rank, heads), F32)],
            done, other_done, where_live, slots_own, slots_other,
            scratch=[pltpu.VMEM((live_slots, wide), BF), pltpu.VMEM((n, cap, side), BF)], name="last",
        )

        def up_gradient(low_ref, g_ref, out_ref):
            low = jnp.concatenate([low_ref[:, :rank], low_ref[:, rank:]], axis=0)
            thrice = dot(jnp.concatenate(split3(low), axis=1), g_ref[...], 0, 0)
            out_ref[...] = adapter_scale * (
                thrice[:rank] + thrice[rank : 2 * rank] + thrice[2 * rank :]
            )

        adapter_up_gradient = call(
            up_gradient, [shape((rank, cols), F32)], low_sum, grad_live,
            flops=6 * live_slots * rank * cols, name="up_gradient",
        )[0]
        return (
            outgoing_residual,
            attention_output_grad,
            down_gradient.T,
            adapter_up_gradient,
            gate_part.reshape(cap),
        )

    return jax.shard_map(
        body,
        mesh=mesh,
        in_specs=(
            P("seq", "tp"),
            P("seq", None),
            P("seq", "tp"),
            P("seq", "tp"),
            P("seq", None),
            P(None, "tp"),
            P("seq"),
            P("seq"),
            P("seq"),
            P("seq", "tp"),
        ),
        out_specs=(P("seq", "tp"), P(None, "seq"), P("seq", None), P(None, "tp"), P("seq")),
        check_vma=False,
    )
```

```python
import functools

import jax
import jax.numpy as jnp
from jax import lax
from jax.experimental import pallas as pl
from jax.experimental.pallas import tpu as pltpu
from jax.sharding import PartitionSpec as P

LEVELS = (
    -1.0,
    -0.6961928009986877,
    -0.5250730514526367,
    -0.39491748809814453,
    -0.28444138169288635,
    -0.18477343022823334,
    -0.09105003625154495,
    0.0,
    0.07958029955625534,
    0.16093020141124725,
    0.24611230194568634,
    0.33791524171829224,
    0.44070982933044434,
    0.5626170039176941,
    0.7229568362236023,
    1.0,
)
adapter_scale = 0.25
BF, F32, I32 = jnp.bfloat16, jnp.float32, jnp.int32
VMEM_LIMIT = 16 * 2**20
DEAD = 2.0


def dot(a, b, ca=1, cb=0):
    return lax.dot_general(a, b, (((ca,), (cb,)), ((), ())), preferred_element_type=F32)


def split2(x):
    hi = x.astype(BF)
    return hi, (x - hi.astype(F32)).astype(BF)


def split3(x):
    hi = x.astype(BF)
    rest = x - hi.astype(F32)
    mid = rest.astype(BF)
    return hi, mid, (rest - mid.astype(F32)).astype(BF)


def call(kernel, outs, *args, flops=0, scratch=(), in_specs=None, name=None):
    nbytes = sum(a.size * a.dtype.itemsize for a in args) + sum(
        o.size * o.dtype.itemsize for o in outs
    )
    whole = pl.BlockSpec(memory_space=pltpu.VMEM)
    return pl.pallas_call(
        kernel,
        out_shape=tuple(outs),
        in_specs=in_specs or [whole] * len(args),
        out_specs=tuple([whole] * len(outs)),
        scratch_shapes=list(scratch),
        compiler_params=pltpu.CompilerParams(vmem_limit_bytes=VMEM_LIMIT),
        cost_estimate=pl.CostEstimate(flops=flops, bytes_accessed=nbytes, transcendentals=0),
        name=name,
    )(*args)


def shape(dims, dtype):
    return jax.ShapeDtypeStruct(tuple(dims), dtype)


def column(row):
    k = row.shape[1]
    eye = lax.broadcasted_iota(I32, (k, k), 0) == lax.broadcasted_iota(I32, (k, k), 1)
    return jnp.sum(jnp.where(eye, row, jnp.zeros_like(row)), axis=1, keepdims=True)


def row_of(col):
    k = col.shape[0]
    eye = lax.broadcasted_iota(I32, (k, k), 0) == lax.broadcasted_iota(I32, (k, k), 1)
    return jnp.sum(jnp.where(eye, col, jnp.zeros_like(col)), axis=0, keepdims=True)


def tree_levels(codes):
    values = list(LEVELS)
    for bit in range(4):
        odd = (codes & (1 << bit)) != 0
        values = [jnp.where(odd, values[2 * i + 1], values[2 * i]) for i in range(len(values) // 2)]
    return values[0]


def dequant_kernel(first, codes_hbm, absmax_ref, *refs):
    weight_ref, token_ref, codes, sems = refs[-4:]
    chunks, block, cols = codes.shape
    blocks = absmax_ref.shape[1]
    per = cols // blocks

    def copy(i):
        rows = pl.ds(first + i * block, block)
        return pltpu.make_async_copy(codes_hbm.at[rows], codes.at[i], sems.at[i])

    for i in range(chunks):
        copy(i).start()
    token_ref[...] = jnp.zeros_like(token_ref)
    column_block = lax.broadcasted_iota(I32, (block, 128), 1) // per

    @pl.loop(0, chunks)
    def _(i):
        rows = pl.ds(pl.multiple_of(i * block, block), block)
        absmax = absmax_ref[pl.ds(pl.multiple_of(first + i * block, block), block), :]
        absmax = jnp.concatenate([absmax] * (128 // blocks), axis=1)
        copy(i).wait()
        for c in range(cols // 128):
            part = slice(c * 128, c * 128 + 128)
            scale = jnp.take_along_axis(absmax, column_block + c * (128 // per), axis=1, mode="promise_in_bounds")
            weight_ref[rows, part] = (tree_levels(codes[i, :, part]) * scale).astype(BF)


def in_hbm(array):
    return pltpu.with_memory_space_constraint(array, pltpu.HBM)


def solution(mesh):
    n, tp = mesh.shape["seq"], mesh.shape["tp"]
    half = n // 2
    order = list(range(0, n, 2)) + list(range(n - 1, 0, -2))

    def ring(step):
        return [(order[i], order[(i + step) % n]) for i in range(n)]

    def flip(size, bit):
        return [(i, i ^ bit) for i in range(size)]

    def place(shard):
        return jnp.where(shard % 2 == 0, shard // 2, n - 1 - shard // 2)

    def shard_at(position):
        position = lax.rem(position + 2 * n, n)
        return jnp.where(position < half, 2 * position, 2 * (n - 1 - position) + 1)

    def body(
        residual,
        attention,
        quantized_codes,
        absmax,
        adapter_down,
        adapter_up,
        routed_slot_gate,
        selected,
        counts,
        cotangent,
    ):
        cap, all_heads = attention.shape
        tokens, cols = residual.shape
        heads = all_heads // n
        rank = adapter_up.shape[0]
        shares = 4 if tp % 4 == 0 and heads % 512 == 0 else 2
        sub = heads // shares
        wsub = heads // 2
        slots = n * cap
        side = 2 * rank
        down_t = adapter_down.T
        gate_row = routed_slot_gate.reshape(1, cap)
        selected_row = selected.reshape(1, cap)
        hbm = pl.BlockSpec(memory_space=pltpu.HBM)
        smem = pl.BlockSpec(memory_space=pltpu.SMEM)
        vmem = pl.BlockSpec(memory_space=pltpu.VMEM)

        def me():
            return lax.axis_index("seq"), lax.axis_index("tp") % 2

        def share():
            return lax.axis_index("tp") % shares

        def live_row(counts_ref):
            return lax.broadcasted_iota(I32, (1, cap), 1) < counts_ref[0]

        def pick(counts_ref, selected_ref):
            at = lax.broadcasted_iota(I32, (tokens, cap), 0) == selected_ref[...]
            return jnp.where(at & live_row(counts_ref), 1.0, 0.0).astype(BF)

        some = slots // 4
        live_slots = slots // 2

        def prepare(counts_ref, selected_ref, gate_ref, attention_ref, cot_ref, send_ref, own_ref, grad_ref, up_ref, chosen, gates, cots, sems):
            seq, _ = me()
            first = [
                pltpu.make_async_copy(selected_ref, chosen, sems.at[0]),
                pltpu.make_async_copy(gate_ref, gates, sems.at[1]),
                pltpu.make_async_copy(cot_ref, cots, sems.at[2]),
            ]
            later = []
            for k in range(half):
                for ref, flipped in ((send_ref, 1), (own_ref, 0)):
                    at = pl.multiple_of((seq ^ (2 * k + flipped)) * heads + share() * sub, 128)
                    sem = sems.at[3 + 2 * k + flipped]
                    later.append(pltpu.make_async_copy(attention_ref.at[:, pl.ds(at, sub)], ref.at[k], sem))
            for copy in first + later:
                copy.start()
            for copy in first:
                copy.wait()
            upstream = dot(pick(counts_ref, chosen), cots[...], 0, 0)
            up_ref[...] = upstream.astype(BF)
            live = column(jnp.where(live_row(counts_ref), 1.0, 0.0)) > 0
            grad_ref[...] = jnp.where(live, column(gates[...]) * upstream, DEAD).astype(BF)
            for copy in later:
                copy.wait()

        send, own, grad, upstream = call(
            prepare,
            [shape((half, cap, sub), BF)] * 2 + [shape((cap, cols), BF)] * 2,
            counts, in_hbm(selected_row), in_hbm(gate_row), in_hbm(attention), in_hbm(cotangent),
            in_specs=[smem] + [hbm] * 4,
            scratch=[
                pltpu.VMEM((1, cap), I32),
                pltpu.VMEM((1, cap), F32),
                pltpu.VMEM((tokens, cols), BF),
                pltpu.SemaphoreType.DMA((3 + n,)),
            ],
            name="prepare",
        )

        across = lax.ppermute(send, "seq", flip(n, 1))
        going, coming = lax.ppermute(grad, "seq", ring(1)), lax.ppermute(grad, "seq", ring(-1))
        block = min(64, wsub)

        def dequantize(part, *after):
            return call(
                functools.partial(dequant_kernel, part * wsub), [shape((wsub, cols), BF), shape((8, 128), F32)],
                in_hbm(quantized_codes), absmax, *after,
                in_specs=[hbm, vmem] + [vmem] * len(after), flops=wsub * cols * 100, name="dequantize",
                scratch=[
                    pltpu.VMEM((wsub // block, block, cols), I32),
                    pltpu.SemaphoreType.DMA((wsub // block,)),
                ],
            )

        weight0, mark = dequantize(0)
        across, going, coming, mark = lax.optimization_barrier((across, going, coming, mark))

        gathered = {0: (grad,)}

        def hop(step, going, coming):
            gathered[n - step], gathered[step] = (going,), (coming,)
            return lax.ppermute(going, "seq", ring(1)), lax.ppermute(coming, "seq", ring(-1))

        def pair(own_ref, across_ref, going_ref, coming_ref, token_ref, *refs):
            *refs, going_out_ref, coming_out_ref, token_out_ref = refs
            for k, ref in enumerate(refs):
                ref[0] = own_ref[k]
                ref[1] = across_ref[k]
            going_out_ref[...] = going_ref[...]
            coming_out_ref[...] = coming_ref[...]
            token_out_ref[...] = token_ref[...]

        def join(*refs):
            *refs, token_ref, out_ref = refs
            for k, ref in enumerate(refs):
                out_ref[2 * k * cap : 2 * (k + 1) * cap, :] = ref[...].reshape(2 * cap, sub)

        *pairs, going, coming, mark = call(
            pair, [shape((2, cap, sub), BF)] * half + [shape((cap, cols), BF)] * 2 + [shape((8, 128), F32)],
            own, across, going, coming, mark, name="pair",
        )
        fetched = [pairs[0]] + [lax.ppermute(pairs[k], "seq", flip(n, 2 * k)) for k in range(1, half)]
        going, coming = hop(1, going, coming)
        mid = cap // 2
        mid = cap // 2
        weight1, mark = dequantize(1, mark)
        weights = weight0, weight1
        fetched, going, coming, mark = lax.optimization_barrier((fetched, going, coming, mark))
        pieces = list(call(join, [shape((slots, sub), BF)], *fetched, mark, name="join"))
        for step in range(2, half - 1):
            going, coming = hop(step, going, coming)
        if shares == 4:
            pieces.append(lax.ppermute(pieces[0], "tp", flip(tp, 2)))
        pieces, going, coming = lax.optimization_barrier((pieces, going, coming))
        others = [lax.ppermute(piece, "tp", flip(tp, 1)) for piece in pieces]
        pieces = [pieces[0], others[0]] + ([pieces[1], others[1]] if shares == 4 else [])
        gathered[n - half + 1], gathered[half - 1] = (going,), (coming,)
        gathered[half] = (
            lax.ppermute(going[:mid], "seq", ring(1)),
            lax.ppermute(coming[mid:], "seq", ring(-1)),
        )

        def natural(refs):
            parts = [ref[...] for ref in refs]
            for bit in (1, 2)[: shares // 2]:
                unset = share() // bit % 2 == 0
                parts = [jnp.where(unset, parts[k], parts[k ^ bit]) for k in range(shares)]
            return jnp.concatenate(parts, axis=1)

        def forward(down_ref, up_ref, w0_ref, w1_ref, *refs):
            piece_refs, (out_ref, low_ref, every) = refs[:shares], refs[shares:]
            seq, _ = me()
            att = natural(piece_refs)
            low = dot(att, down_ref[...], 1, 1)
            thrice = jnp.concatenate(split3(adapter_scale * low), axis=1)
            for j in range(n):
                every[seq ^ j] = low[j * cap : (j + 1) * cap]
            top, bottom = every[:half].reshape(live_slots, rank), every[half:].reshape(live_slots, rank)
            low_ref[...] = jnp.concatenate([top, bottom], axis=1)
            spots = [lax.rem(place(seq ^ j) - place(seq) + n, n) for j in range(n)]
            tile = min(512, cols)
            for c in range(cols // tile):
                part = slice(c * tile, (c + 1) * tile)
                ups = up_ref[:, part]
                acc = dot(thrice, jnp.concatenate([ups] * 3, axis=0))
                acc = acc + dot(att[:, :wsub], w0_ref[:, part]) + dot(att[:, wsub:], w1_ref[:, part])
                acc = acc.astype(BF)
                for j in range(n):
                    out_ref[spots[j], :, part] = acc[j * cap : (j + 1) * cap]

        partial, low = call(
            forward,
            [shape((n, cap, cols), BF), shape((live_slots, side), F32)],
            down_t, adapter_up, *weights, *pieces,
            flops=2 * slots * heads * cols, name="forward", scratch=[pltpu.VMEM((n, cap, rank), F32)],
        )

        here, there = partial[half, :mid], partial[half, mid:]
        first_step = lax.ppermute(here, "seq", ring(1)), lax.ppermute(there, "seq", ring(-1))
        low_across = lax.ppermute(low, "seq", flip(n, 1))
        spots = [r for r in range(n) if r != half]

        def backward(up_ref, w0_ref, w1_ref, first_ref, second_ref, *refs):
            g_refs, (keep_ref, send_ref, live_ref, where_ref, every, sums) = refs[: n - 1], refs[n - 1 :]
            seq, core = me()
            for r, ref in zip(spots, g_refs):
                every[shard_at(place(seq) + r)] = ref[...]
            every[shard_at(place(seq) + half)] = jnp.concatenate([first_ref[...], second_ref[...]])
            passed = jnp.zeros((1, 1), F32)
            row = lax.broadcasted_iota(I32, (cap, live_slots), 0).astype(F32)
            col = lax.broadcasted_iota(I32, (cap, live_slots), 1).astype(F32)
            for j in range(n):
                alive = jnp.where(every[j][:, :1].astype(F32) < 0.5 * (1 + DEAD), 1.0, 0.0)
                at = jnp.where((row + passed == col) & (alive > 0), 1.0, 0.0)
                where_ref[j * cap : (j + 1) * cap, :] = at.astype(BF)
                passed = passed + jnp.sum(alive, axis=0, keepdims=True)
            g = dot(where_ref[...], every[...].reshape(slots, cols), 0, 0).astype(BF)
            live_ref[...] = g
            tile = min(256, wsub)
            for i in range(wsub // tile):
                for at, ref in ((0, w0_ref), (wsub, w1_ref)):
                    sums[:, at + i * tile : at + (i + 1) * tile] = dot(g, ref[i * tile : (i + 1) * tile, :], 1, 1)
            hi, lo = split2(adapter_scale * dot(g, up_ref[...], 1, 1))
            sums[:, heads:] = jnp.concatenate([hi, lo], axis=1).astype(F32)
            keep_ref[...] = sums[pl.ds(pl.multiple_of(core * some, 8), some), :]
            send_ref[...] = sums[pl.ds(pl.multiple_of((1 - core) * some, 8), some), :].astype(BF)

        def compact(low_ref, low_across_ref, where_ref, out_ref):
            low = low_ref[...] + low_across_ref[...]
            low = jnp.concatenate([low[:, :rank], low[:, rank:]], axis=0)
            low = dot(where_ref[...], jnp.concatenate(split3(low), axis=1), 0, 0)
            low = low[:, :rank] + low[:, rank : 2 * rank] + low[:, 2 * rank :]
            out_ref[...] = jnp.concatenate([low[: live_slots // 2], low[live_slots // 2 :]], axis=1)

        wide = heads + side

        def back(*farthest):
            return call(
                backward,
                [
                    shape((some, wide), F32),
                    shape((some, wide), BF),
                    shape((live_slots, cols), BF),
                    shape((slots, live_slots), BF),
                ],
                adapter_up, *weights, *farthest, *[gathered[r][0] for r in spots],
                flops=2 * live_slots * heads * cols,
                scratch=[pltpu.VMEM((n, cap, cols), BF), pltpu.VMEM((live_slots, wide), F32)],
                name="backward",
            )

        def ranks(a, b):
            return (a[:, heads : heads + rank].astype(F32) + b[:, heads : heads + rank].astype(F32)) + (
                a[:, heads + rank :].astype(F32) + b[:, heads + rank :].astype(F32)
            )

        def add(a_ref, b_ref, out_ref):
            a, b = a_ref[...], b_ref[...]
            out_ref[:, :heads] = (a[:, :heads].astype(F32) + b[:, :heads].astype(F32)).astype(BF)
            out_ref[:, heads:] = jnp.concatenate(split2(ranks(a, b)), axis=1)

        def finish(a_ref, b_ref, down_ref, out_ref):
            a, b = a_ref[...], b_ref[...]
            rank_grad = ranks(a, b).astype(BF)
            tail = dot(rank_grad, down_ref[...])
            out_ref[:, :heads] = (a[:, :heads].astype(F32) + b[:, :heads].astype(F32) + tail).astype(BF)
            out_ref[:, heads:] = jnp.concatenate([rank_grad, jnp.zeros_like(rank_grad)], axis=1)

        def plus(a, b):
            return (a.astype(F32) + b.astype(F32)).astype(BF)

        def sum_heads(keep, send):
            recv = yield lax.ppermute(send, "tp", flip(tp, 1))
            mine = call(add, [shape((some, wide), BF)], keep, recv, name="add")[0]
            bit = 2
            while 2 * bit < tp:
                recv = yield lax.ppermute(mine, "tp", flip(tp, bit))
                mine = call(add, [shape((some, wide), BF)], mine, recv, name="add")[0]
                bit *= 2
            recv = yield lax.ppermute(mine, "tp", flip(tp, bit))
            done = call(finish, [shape((some, wide), BF)], mine, recv, down_t, name="finish")[0]
            other_done = yield lax.ppermute(done, "tp", flip(tp, 1))
            return done, other_done

        def sum_low(total):
            bit = half
            while bit > 1:
                recv = yield lax.ppermute(total, "seq", flip(n, bit))
                total = total + recv
                bit //= 2
            return total

        def drain(steps, value):
            try:
                while True:
                    value = steps.send(value)
            except StopIteration as stop:
                return stop.value

        going, coming = first_step
        for step in range(half - 1, 0, -1):
            here, there = partial[step], partial[n - step]
            if step == half - 1:
                here = jnp.concatenate([plus(here[:mid], going), here[mid:]])
                there = jnp.concatenate([there[:mid], plus(there[mid:], coming)])
                keep, send, grad_live, where_live = back(*gathered[half])
                here, there, send = lax.optimization_barrier((here, there, send))
            else:
                here, there = plus(here, going), plus(there, coming)
                if step == half - 2:
                    here, there, head_value, low_across = lax.optimization_barrier((here, there, head_value, low_across))
                else:
                    here, there = lax.optimization_barrier((here, there))
            going = lax.ppermute(here, "seq", ring(1))
            coming = lax.ppermute(there, "seq", ring(-1))
            if step == half - 1:
                head_steps, head_value = sum_heads(keep, send), None
            elif step == half - 2:
                low_live = call(compact, [shape((some, side), F32)], low, low_across, where_live, name="compact")[0]
                low_steps, low_value = sum_low(low_live), None
                low_value = low_steps.send(None)
            if step >= half - 2:
                head_value = head_steps.send(head_value)
        done, other_done = drain(head_steps, head_value)
        going, coming, other_done, low_value = lax.optimization_barrier((going, coming, other_done, low_value))
        low_sum = drain(low_steps, low_value)

        def home(counts_ref, selected_ref, gate_ref, res_ref, own_ref, going_ref, coming_ref, up_ref, out_ref, gate_out_ref):
            chosen = pick(counts_ref, selected_ref)
            block = own_ref[...].astype(F32) + going_ref[...].astype(F32) + coming_ref[...].astype(F32)
            gate_out_ref[...] = row_of(jnp.sum(up_ref[...].astype(F32) * block, axis=1, keepdims=True))
            res = res_ref[...]
            picked = dot(chosen, res, 0, 0)
            updated = (picked + column(gate_ref[...]) * block).astype(BF)
            hit = jnp.sum(chosen.astype(F32), axis=1, keepdims=True) > 0
            out_ref[...] = jnp.where(hit, dot(chosen, updated), res.astype(F32)).astype(BF)

        outgoing_residual, gate_part = call(
            home,
            [shape((tokens, cols), BF), shape((1, cap), F32)],
            counts, selected_row, gate_row, residual, partial[0], going, coming, upstream,
            in_specs=[smem] + [vmem] * 7, name="home",
        )
        bit = 1
        while bit < tp:
            gate_part = gate_part + lax.ppermute(gate_part, "tp", flip(tp, bit))
            bit *= 2

        def last(a_ref, b_ref, where_ref, *refs):
            piece_refs, (grad_ref, down_grad_ref, live, rank_ref) = refs[:shares], refs[shares:]
            seq, core = me()
            for ref, at in ((a_ref, core), (b_ref, 1 - core)):
                live[pl.ds(pl.multiple_of(at * some, 16), some), :] = ref[...]
            every = dot(where_ref[...], live[...]).astype(BF)
            grad_ref[...] = every[:, :heads]
            for j in range(n):
                rank_ref[j] = every[j * cap : (j + 1) * cap, heads:]
            rank_grad = jnp.concatenate([rank_ref[seq ^ j] for j in range(n)], axis=0)[:, :rank]
            for j, ref in enumerate(piece_refs):
                at = pl.multiple_of((share() ^ j) * sub, 128)
                down_grad_ref[:, pl.ds(at, sub)] = dot(rank_grad, ref[...], 0, 0)

        attention_output_grad, down_gradient = call(
            last,
            [shape((slots, heads), BF), shape((rank, heads), F32)],
            done, other_done, where_live, *pieces,
            scratch=[pltpu.VMEM((live_slots, wide), BF), pltpu.VMEM((n, cap, side), BF)], name="last",
        )

        def up_gradient(low_ref, g_ref, out_ref):
            low = jnp.concatenate([low_ref[:, :rank], low_ref[:, rank:]], axis=0)
            thrice = dot(jnp.concatenate(split3(low), axis=1), g_ref[...], 0, 0)
            out_ref[...] = adapter_scale * (
                thrice[:rank] + thrice[rank : 2 * rank] + thrice[2 * rank :]
            )

        adapter_up_gradient = call(
            up_gradient, [shape((rank, cols), F32)], low_sum, grad_live,
            flops=6 * live_slots * rank * cols, name="up_gradient",
        )[0]
        return (
            outgoing_residual,
            attention_output_grad,
            down_gradient.T,
            adapter_up_gradient,
            gate_part.reshape(cap),
        )

    return jax.shard_map(
        body,
        mesh=mesh,
        in_specs=(
            P("seq", "tp"),
            P("seq", None),
            P("seq", "tp"),
            P("seq", "tp"),
            P("seq", None),
            P(None, "tp"),
            P("seq"),
            P("seq"),
            P("seq"),
            P("seq", "tp"),
        ),
        out_specs=(P("seq", "tp"), P(None, "seq"), P("seq", None), P(None, "tp"), P("seq")),
        check_vma=False,
    )
```

```python
import functools

import jax
import jax.numpy as jnp
from jax import lax
from jax.experimental import pallas as pl
from jax.experimental.pallas import tpu as pltpu
from jax.sharding import PartitionSpec as P

LEVELS = (
    -1.0,
    -0.6961928009986877,
    -0.5250730514526367,
    -0.39491748809814453,
    -0.28444138169288635,
    -0.18477343022823334,
    -0.09105003625154495,
    0.0,
    0.07958029955625534,
    0.16093020141124725,
    0.24611230194568634,
    0.33791524171829224,
    0.44070982933044434,
    0.5626170039176941,
    0.7229568362236023,
    1.0,
)
adapter_scale = 0.25
BF, F32, I32 = jnp.bfloat16, jnp.float32, jnp.int32
VMEM_LIMIT = 16 * 2**20
DEAD = 2.0


def dot(a, b, ca=1, cb=0):
    return lax.dot_general(a, b, (((ca,), (cb,)), ((), ())), preferred_element_type=F32)


def split2(x):
    hi = x.astype(BF)
    return hi, (x - hi.astype(F32)).astype(BF)


def split3(x):
    hi = x.astype(BF)
    rest = x - hi.astype(F32)
    mid = rest.astype(BF)
    return hi, mid, (rest - mid.astype(F32)).astype(BF)


def call(kernel, outs, *args, flops=0, scratch=(), in_specs=None, name=None):
    nbytes = sum(a.size * a.dtype.itemsize for a in args) + sum(
        o.size * o.dtype.itemsize for o in outs
    )
    whole = pl.BlockSpec(memory_space=pltpu.VMEM)
    return pl.pallas_call(
        kernel,
        out_shape=tuple(outs),
        in_specs=in_specs or [whole] * len(args),
        out_specs=tuple([whole] * len(outs)),
        scratch_shapes=list(scratch),
        compiler_params=pltpu.CompilerParams(vmem_limit_bytes=VMEM_LIMIT),
        cost_estimate=pl.CostEstimate(flops=flops, bytes_accessed=nbytes, transcendentals=0),
        name=name,
    )(*args)


def shape(dims, dtype):
    return jax.ShapeDtypeStruct(tuple(dims), dtype)


def column(row):
    k = row.shape[1]
    eye = lax.broadcasted_iota(I32, (k, k), 0) == lax.broadcasted_iota(I32, (k, k), 1)
    return jnp.sum(jnp.where(eye, row, jnp.zeros_like(row)), axis=1, keepdims=True)


def row_of(col):
    k = col.shape[0]
    eye = lax.broadcasted_iota(I32, (k, k), 0) == lax.broadcasted_iota(I32, (k, k), 1)
    return jnp.sum(jnp.where(eye, col, jnp.zeros_like(col)), axis=0, keepdims=True)


def tree_levels(codes):
    values = list(LEVELS)
    for bit in range(4):
        odd = (codes & (1 << bit)) != 0
        values = [jnp.where(odd, values[2 * i + 1], values[2 * i]) for i in range(len(values) // 2)]
    return values[0]


def dequant_kernel(first, codes_hbm, absmax_ref, *refs):
    weight_ref, token_ref, codes, sems = refs[-4:]
    chunks, block, cols = codes.shape
    blocks = absmax_ref.shape[1]
    per = cols // blocks

    def copy(i):
        rows = pl.ds(first + i * block, block)
        return pltpu.make_async_copy(codes_hbm.at[rows], codes.at[i], sems.at[i])

    for i in range(chunks):
        copy(i).start()
    token_ref[...] = jnp.zeros_like(token_ref)
    column_block = lax.broadcasted_iota(I32, (block, 128), 1) // per

    @pl.loop(0, chunks)
    def _(i):
        rows = pl.ds(pl.multiple_of(i * block, block), block)
        absmax = absmax_ref[pl.ds(pl.multiple_of(first + i * block, block), block), :]
        absmax = jnp.concatenate([absmax] * (128 // blocks), axis=1)
        copy(i).wait()
        for c in range(cols // 128):
            part = slice(c * 128, c * 128 + 128)
            scale = jnp.take_along_axis(absmax, column_block + c * (128 // per), axis=1, mode="promise_in_bounds")
            weight_ref[rows, part] = (tree_levels(codes[i, :, part]) * scale).astype(BF)


def in_hbm(array):
    return pltpu.with_memory_space_constraint(array, pltpu.HBM)


def solution(mesh):
    n, tp = mesh.shape["seq"], mesh.shape["tp"]
    half = n // 2
    order = list(range(0, n, 2)) + list(range(n - 1, 0, -2))

    def ring(step):
        return [(order[i], order[(i + step) % n]) for i in range(n)]

    def flip(size, bit):
        return [(i, i ^ bit) for i in range(size)]

    def place(shard):
        return jnp.where(shard % 2 == 0, shard // 2, n - 1 - shard // 2)

    def shard_at(position):
        position = lax.rem(position + 2 * n, n)
        return jnp.where(position < half, 2 * position, 2 * (n - 1 - position) + 1)

    def body(
        residual,
        attention,
        quantized_codes,
        absmax,
        adapter_down,
        adapter_up,
        routed_slot_gate,
        selected,
        counts,
        cotangent,
    ):
        cap, all_heads = attention.shape
        tokens, cols = residual.shape
        heads = all_heads // n
        rank = adapter_up.shape[0]
        shares = 4 if tp % 4 == 0 and heads % 512 == 0 else 2
        sub = heads // shares
        wsub = heads // 2
        slots = n * cap
        side = 2 * rank
        down_t = adapter_down.T
        gate_row = routed_slot_gate.reshape(1, cap)
        selected_row = selected.reshape(1, cap)
        hbm = pl.BlockSpec(memory_space=pltpu.HBM)
        smem = pl.BlockSpec(memory_space=pltpu.SMEM)
        vmem = pl.BlockSpec(memory_space=pltpu.VMEM)

        def me():
            return lax.axis_index("seq"), lax.axis_index("tp") % 2

        def share():
            return lax.axis_index("tp") % shares

        def live_row(counts_ref):
            return lax.broadcasted_iota(I32, (1, cap), 1) < counts_ref[0]

        def pick(counts_ref, selected_ref):
            at = lax.broadcasted_iota(I32, (tokens, cap), 0) == selected_ref[...]
            return jnp.where(at & live_row(counts_ref), 1.0, 0.0).astype(BF)

        some = slots // 4
        live_slots = slots // 2

        def prepare(counts_ref, selected_ref, gate_ref, attention_ref, cot_ref, send_ref, own_ref, grad_ref, up_ref, chosen, gates, cots, sems):
            seq, _ = me()
            first = [
                pltpu.make_async_copy(selected_ref, chosen, sems.at[0]),
                pltpu.make_async_copy(gate_ref, gates, sems.at[1]),
                pltpu.make_async_copy(cot_ref, cots, sems.at[2]),
            ]
            later = []
            for k in range(half):
                for ref, flipped in ((send_ref, 1), (own_ref, 0)):
                    at = pl.multiple_of((seq ^ (2 * k + flipped)) * heads + share() * sub, 128)
                    sem = sems.at[3 + 2 * k + flipped]
                    later.append(pltpu.make_async_copy(attention_ref.at[:, pl.ds(at, sub)], ref.at[k], sem))
            for copy in first + later:
                copy.start()
            for copy in first:
                copy.wait()
            upstream = dot(pick(counts_ref, chosen), cots[...], 0, 0)
            up_ref[...] = upstream.astype(BF)
            live = column(jnp.where(live_row(counts_ref), 1.0, 0.0)) > 0
            grad_ref[...] = jnp.where(live, column(gates[...]) * upstream, DEAD).astype(BF)
            for copy in later:
                copy.wait()

        send, own, grad, upstream = call(
            prepare,
            [shape((half, cap, sub), BF)] * 2 + [shape((cap, cols), BF)] * 2,
            counts, in_hbm(selected_row), in_hbm(gate_row), in_hbm(attention), in_hbm(cotangent),
            in_specs=[smem] + [hbm] * 4,
            scratch=[
                pltpu.VMEM((1, cap), I32),
                pltpu.VMEM((1, cap), F32),
                pltpu.VMEM((tokens, cols), BF),
                pltpu.SemaphoreType.DMA((3 + n,)),
            ],
            name="prepare",
        )

        across = lax.ppermute(send, "seq", flip(n, 1))
        going, coming = lax.ppermute(grad, "seq", ring(1)), lax.ppermute(grad, "seq", ring(-1))
        block = min(64, wsub)

        def dequantize(part, *after):
            return call(
                functools.partial(dequant_kernel, part * wsub), [shape((wsub, cols), BF), shape((8, 128), F32)],
                in_hbm(quantized_codes), absmax, *after,
                in_specs=[hbm, vmem] + [vmem] * len(after), flops=wsub * cols * 100, name="dequantize",
                scratch=[
                    pltpu.VMEM((wsub // block, block, cols), I32),
                    pltpu.SemaphoreType.DMA((wsub // block,)),
                ],
            )

        weight0, mark = dequantize(0)
        across, going, coming, mark = lax.optimization_barrier((across, going, coming, mark))

        gathered = {0: (grad,)}

        def hop(step, going, coming):
            gathered[n - step], gathered[step] = (going,), (coming,)
            return lax.ppermute(going, "seq", ring(1)), lax.ppermute(coming, "seq", ring(-1))

        def pair(own_ref, across_ref, going_ref, coming_ref, token_ref, *refs):
            *refs, going_out_ref, coming_out_ref, token_out_ref = refs
            for k, ref in enumerate(refs):
                ref[0] = own_ref[k]
                ref[1] = across_ref[k]
            going_out_ref[...] = going_ref[...]
            coming_out_ref[...] = coming_ref[...]
            token_out_ref[...] = token_ref[...]

        def join(*refs):
            *refs, token_ref, out_ref = refs
            for k, ref in enumerate(refs):
                out_ref[2 * k * cap : 2 * (k + 1) * cap, :] = ref[...].reshape(2 * cap, sub)

        *pairs, going, coming, mark = call(
            pair, [shape((2, cap, sub), BF)] * half + [shape((cap, cols), BF)] * 2 + [shape((8, 128), F32)],
            own, across, going, coming, mark, name="pair",
        )
        fetched = [pairs[0]] + [lax.ppermute(pairs[k], "seq", flip(n, 2 * k)) for k in range(1, half)]
        going, coming = hop(1, going, coming)
        mid = cap // 2
        mid = cap // 2
        weight1, mark = dequantize(1, mark)
        weights = weight0, weight1
        fetched, going, coming, mark = lax.optimization_barrier((fetched, going, coming, mark))
        pieces = list(call(join, [shape((slots, sub), BF)], *fetched, mark, name="join"))
        for step in range(2, half - 1):
            going, coming = hop(step, going, coming)
        if shares == 4:
            pieces.append(lax.ppermute(pieces[0], "tp", flip(tp, 2)))
        pieces, going, coming = lax.optimization_barrier((pieces, going, coming))
        others = [lax.ppermute(piece, "tp", flip(tp, 1)) for piece in pieces]
        pieces = [pieces[0], others[0]] + ([pieces[1], others[1]] if shares == 4 else [])
        gathered[n - half + 1], gathered[half - 1] = (going,), (coming,)
        gathered[half] = (
            lax.ppermute(going[:mid], "seq", ring(1)),
            lax.ppermute(coming[mid:], "seq", ring(-1)),
        )

        def natural(refs):
            parts = [ref[...] for ref in refs]
            for bit in (1, 2)[: shares // 2]:
                unset = share() // bit % 2 == 0
                parts = [jnp.where(unset, parts[k], parts[k ^ bit]) for k in range(shares)]
            return jnp.concatenate(parts, axis=1)

        def forward(down_ref, up_ref, w0_ref, w1_ref, *refs):
            piece_refs, (out_ref, low_ref, every) = refs[:shares], refs[shares:]
            seq, _ = me()
            att = natural(piece_refs)
            low = dot(att, down_ref[...], 1, 1)
            thrice = jnp.concatenate(split3(adapter_scale * low), axis=1)
            for j in range(n):
                every[seq ^ j] = low[j * cap : (j + 1) * cap]
            top, bottom = every[:half].reshape(live_slots, rank), every[half:].reshape(live_slots, rank)
            low_ref[...] = jnp.concatenate([top, bottom], axis=1)
            spots = [lax.rem(place(seq ^ j) - place(seq) + n, n) for j in range(n)]
            tile = min(512, cols)
            for c in range(cols // tile):
                part = slice(c * tile, (c + 1) * tile)
                ups = up_ref[:, part]
                acc = dot(thrice, jnp.concatenate([ups] * 3, axis=0))
                acc = acc + dot(att[:, :wsub], w0_ref[:, part]) + dot(att[:, wsub:], w1_ref[:, part])
                acc = acc.astype(BF)
                for j in range(n):
                    out_ref[spots[j], :, part] = acc[j * cap : (j + 1) * cap]

        partial, low = call(
            forward,
            [shape((n, cap, cols), BF), shape((live_slots, side), F32)],
            down_t, adapter_up, *weights, *pieces,
            flops=2 * slots * heads * cols, name="forward", scratch=[pltpu.VMEM((n, cap, rank), F32)],
        )

        here, there = partial[half, :mid], partial[half, mid:]
        first_step = lax.ppermute(here, "seq", ring(1)), lax.ppermute(there, "seq", ring(-1))
        low_across = lax.ppermute(low, "seq", flip(n, 1))
        spots = [r for r in range(n) if r != half]

        def backward(up_ref, w0_ref, w1_ref, first_ref, second_ref, *refs):
            g_refs, (keep_ref, send_ref, live_ref, where_ref, every, sums) = refs[: n - 1], refs[n - 1 :]
            seq, core = me()
            for r, ref in zip(spots, g_refs):
                every[shard_at(place(seq) + r)] = ref[...]
            every[shard_at(place(seq) + half)] = jnp.concatenate([first_ref[...], second_ref[...]])
            passed = jnp.zeros((1, 1), F32)
            row = lax.broadcasted_iota(I32, (cap, live_slots), 0).astype(F32)
            col = lax.broadcasted_iota(I32, (cap, live_slots), 1).astype(F32)
            for j in range(n):
                alive = jnp.where(every[j][:, :1].astype(F32) < 0.5 * (1 + DEAD), 1.0, 0.0)
                at = jnp.where((row + passed == col) & (alive > 0), 1.0, 0.0)
                where_ref[j * cap : (j + 1) * cap, :] = at.astype(BF)
                passed = passed + jnp.sum(alive, axis=0, keepdims=True)
            g = dot(where_ref[...], every[...].reshape(slots, cols), 0, 0).astype(BF)
            live_ref[...] = g
            tile = min(256, wsub)
            for i in range(wsub // tile):
                for at, ref in ((0, w0_ref), (wsub, w1_ref)):
                    sums[:, at + i * tile : at + (i + 1) * tile] = dot(g, ref[i * tile : (i + 1) * tile, :], 1, 1)
            hi, lo = split2(adapter_scale * dot(g, up_ref[...], 1, 1))
            sums[:, heads:] = jnp.concatenate([hi, lo], axis=1).astype(F32)
            keep_ref[...] = sums[pl.ds(pl.multiple_of(core * some, 8), some), :]
            send_ref[...] = sums[pl.ds(pl.multiple_of((1 - core) * some, 8), some), :].astype(BF)

        def compact(low_ref, low_across_ref, where_ref, out_ref):
            low = low_ref[...] + low_across_ref[...]
            low = jnp.concatenate([low[:, :rank], low[:, rank:]], axis=0)
            low = dot(where_ref[...], jnp.concatenate(split3(low), axis=1), 0, 0)
            low = low[:, :rank] + low[:, rank : 2 * rank] + low[:, 2 * rank :]
            out_ref[...] = jnp.concatenate([low[: live_slots // 2], low[live_slots // 2 :]], axis=1)

        wide = heads + side

        def back(*farthest):
            return call(
                backward,
                [
                    shape((some, wide), F32),
                    shape((some, wide), BF),
                    shape((live_slots, cols), BF),
                    shape((slots, live_slots), BF),
                ],
                adapter_up, *weights, *farthest, *[gathered[r][0] for r in spots],
                flops=2 * live_slots * heads * cols,
                scratch=[pltpu.VMEM((n, cap, cols), BF), pltpu.VMEM((live_slots, wide), F32)],
                name="backward",
            )

        def ranks(a, b):
            return (a[:, heads : heads + rank].astype(F32) + b[:, heads : heads + rank].astype(F32)) + (
                a[:, heads + rank :].astype(F32) + b[:, heads + rank :].astype(F32)
            )

        def add(a_ref, b_ref, out_ref):
            a, b = a_ref[...], b_ref[...]
            out_ref[:, :heads] = (a[:, :heads].astype(F32) + b[:, :heads].astype(F32)).astype(BF)
            out_ref[:, heads:] = jnp.concatenate(split2(ranks(a, b)), axis=1)

        def finish(a_ref, b_ref, down_ref, low_ref, low_other_ref, out_ref, low_out_ref):
            low_out_ref[...] = low_ref[...] + low_other_ref[...]
            a, b = a_ref[...], b_ref[...]
            rank_grad = ranks(a, b).astype(BF)
            tail = dot(rank_grad, down_ref[...])
            out_ref[:, :heads] = (a[:, :heads].astype(F32) + b[:, :heads].astype(F32) + tail).astype(BF)
            out_ref[:, heads:] = jnp.concatenate([rank_grad, jnp.zeros_like(rank_grad)], axis=1)

        def plus(a, b):
            return (a.astype(F32) + b.astype(F32)).astype(BF)

        def sum_heads(keep, send):
            recv = yield lax.ppermute(send, "tp", flip(tp, 1))
            mine = call(add, [shape((some, wide), BF)], keep, recv, name="add")[0]
            bit = 2
            while 2 * bit < tp:
                recv = yield lax.ppermute(mine, "tp", flip(tp, bit))
                mine = call(add, [shape((some, wide), BF)], mine, recv, name="add")[0]
                bit *= 2
            recv = yield lax.ppermute(mine, "tp", flip(tp, bit))
            done, low_total = call(
                finish, [shape((some, wide), BF), shape((live_slots // 2, side), F32)],
                mine, recv, down_t, *low_terms, name="finish",
            )
            other_done = yield lax.ppermute(done, "tp", flip(tp, 1))
            return done, other_done, low_total

        def sum_low(total):
            bit = half // 2
            while bit > 1:
                recv = yield lax.ppermute(total, "seq", flip(n, bit))
                total = total + recv
                bit //= 2
            return total

        def drain(steps, value):
            try:
                while True:
                    value = steps.send(value)
            except StopIteration as stop:
                return stop.value

        going, coming = first_step
        for step in range(half - 1, 0, -1):
            here, there = partial[step], partial[n - step]
            if step == half - 1:
                here = jnp.concatenate([plus(here[:mid], going), here[mid:]])
                there = jnp.concatenate([there[:mid], plus(there[mid:], coming)])
                keep, send, grad_live, where_live = back(*gathered[half])
                here, there, send = lax.optimization_barrier((here, there, send))
            else:
                here, there = plus(here, going), plus(there, coming)
                if step == half - 2:
                    here, there, head_value, low_across = lax.optimization_barrier((here, there, head_value, low_across))
                else:
                    here, there = lax.optimization_barrier((here, there))
            going = lax.ppermute(here, "seq", ring(1))
            coming = lax.ppermute(there, "seq", ring(-1))
            if step == half - 1:
                head_steps, head_value = sum_heads(keep, send), None
            elif step == half - 2:
                low_live = call(compact, [shape((some, side), F32)], low, low_across, where_live, name="compact")[0]
                low_terms = low_live, lax.ppermute(low_live, "seq", flip(n, half))
            if step >= half - 2:
                head_value = head_steps.send(head_value)
        done, other_done, low_total = drain(head_steps, head_value)
        low_steps = sum_low(low_total)
        low_value = low_steps.send(None)
        def last(a_ref, b_ref, where_ref, *refs):
            piece_refs, (grad_ref, down_grad_ref, token_ref, live, rank_ref) = refs[:shares], refs[shares:]
            token_ref[...] = jnp.zeros_like(token_ref)
            seq, core = me()
            for ref, at in ((a_ref, core), (b_ref, 1 - core)):
                live[pl.ds(pl.multiple_of(at * some, 16), some), :] = ref[...]
            every = dot(where_ref[...], live[...]).astype(BF)
            grad_ref[...] = every[:, :heads]
            for j in range(n):
                rank_ref[j] = every[j * cap : (j + 1) * cap, heads:]
            rank_grad = jnp.concatenate([rank_ref[seq ^ j] for j in range(n)], axis=0)[:, :rank]
            for j, ref in enumerate(piece_refs):
                at = pl.multiple_of((share() ^ j) * sub, 128)
                down_grad_ref[:, pl.ds(at, sub)] = dot(rank_grad, ref[...], 0, 0)

        attention_output_grad, down_gradient, mark = call(
            last,
            [shape((slots, heads), BF), shape((rank, heads), F32), shape((8, 128), F32)],
            done, other_done, where_live, *pieces,
            scratch=[pltpu.VMEM((live_slots, wide), BF), pltpu.VMEM((n, cap, side), BF)], name="last",
        )

        going, coming, mark, low_value = lax.optimization_barrier((going, coming, mark, low_value))
        low_sum = drain(low_steps, low_value)

        def home(counts_ref, selected_ref, gate_ref, res_ref, own_ref, going_ref, coming_ref, up_ref, _, out_ref, gate_out_ref):
            chosen = pick(counts_ref, selected_ref)
            block = own_ref[...].astype(F32) + going_ref[...].astype(F32) + coming_ref[...].astype(F32)
            gate_out_ref[...] = row_of(jnp.sum(up_ref[...].astype(F32) * block, axis=1, keepdims=True))
            res = res_ref[...]
            picked = dot(chosen, res, 0, 0)
            updated = (picked + column(gate_ref[...]) * block).astype(BF)
            hit = jnp.sum(chosen.astype(F32), axis=1, keepdims=True) > 0
            out_ref[...] = jnp.where(hit, dot(chosen, updated), res.astype(F32)).astype(BF)

        outgoing_residual, gate_part = call(
            home,
            [shape((tokens, cols), BF), shape((1, cap), F32)],
            counts, selected_row, gate_row, residual, partial[0], going, coming, upstream, mark,
            in_specs=[smem] + [vmem] * 8, name="home",
        )
        bit = 1
        while bit < tp:
            gate_part = gate_part + lax.ppermute(gate_part, "tp", flip(tp, bit))
            bit *= 2

        def up_gradient(low_ref, g_ref, out_ref):
            low = jnp.concatenate([low_ref[:, :rank], low_ref[:, rank:]], axis=0)
            thrice = dot(jnp.concatenate(split3(low), axis=1), g_ref[...], 0, 0)
            out_ref[...] = adapter_scale * (
                thrice[:rank] + thrice[rank : 2 * rank] + thrice[2 * rank :]
            )

        adapter_up_gradient = call(
            up_gradient, [shape((rank, cols), F32)], low_sum, grad_live,
            flops=6 * live_slots * rank * cols, name="up_gradient",
        )[0]
        return (
            outgoing_residual,
            attention_output_grad,
            down_gradient.T,
            adapter_up_gradient,
            gate_part.reshape(cap),
        )

    return jax.shard_map(
        body,
        mesh=mesh,
        in_specs=(
            P("seq", "tp"),
            P("seq", None),
            P("seq", "tp"),
            P("seq", "tp"),
            P("seq", None),
            P(None, "tp"),
            P("seq"),
            P("seq"),
            P("seq"),
            P("seq", "tp"),
        ),
        out_specs=(P("seq", "tp"), P(None, "seq"), P("seq", None), P(None, "tp"), P("seq")),
        check_vma=False,
    )
```

```python
import functools

import jax
import jax.numpy as jnp
from jax import lax
from jax.experimental import pallas as pl
from jax.experimental.pallas import tpu as pltpu
from jax.sharding import PartitionSpec as P

LEVELS = (
    -1.0,
    -0.6961928009986877,
    -0.5250730514526367,
    -0.39491748809814453,
    -0.28444138169288635,
    -0.18477343022823334,
    -0.09105003625154495,
    0.0,
    0.07958029955625534,
    0.16093020141124725,
    0.24611230194568634,
    0.33791524171829224,
    0.44070982933044434,
    0.5626170039176941,
    0.7229568362236023,
    1.0,
)
adapter_scale = 0.25
BF, F32, I32 = jnp.bfloat16, jnp.float32, jnp.int32
VMEM_LIMIT = 16 * 2**20
DEAD = 2.0


def dot(a, b, ca=1, cb=0):
    return lax.dot_general(a, b, (((ca,), (cb,)), ((), ())), preferred_element_type=F32)


def split2(x):
    hi = x.astype(BF)
    return hi, (x - hi.astype(F32)).astype(BF)


def split3(x):
    hi = x.astype(BF)
    rest = x - hi.astype(F32)
    mid = rest.astype(BF)
    return hi, mid, (rest - mid.astype(F32)).astype(BF)


def call(kernel, outs, *args, flops=0, scratch=(), in_specs=None, name=None):
    nbytes = sum(a.size * a.dtype.itemsize for a in args) + sum(
        o.size * o.dtype.itemsize for o in outs
    )
    whole = pl.BlockSpec(memory_space=pltpu.VMEM)
    return pl.pallas_call(
        kernel,
        out_shape=tuple(outs),
        in_specs=in_specs or [whole] * len(args),
        out_specs=tuple([whole] * len(outs)),
        scratch_shapes=list(scratch),
        compiler_params=pltpu.CompilerParams(vmem_limit_bytes=VMEM_LIMIT),
        cost_estimate=pl.CostEstimate(flops=flops, bytes_accessed=nbytes, transcendentals=0),
        name=name,
    )(*args)


def shape(dims, dtype):
    return jax.ShapeDtypeStruct(tuple(dims), dtype)


def column(row):
    k = row.shape[1]
    eye = lax.broadcasted_iota(I32, (k, k), 0) == lax.broadcasted_iota(I32, (k, k), 1)
    return jnp.sum(jnp.where(eye, row, jnp.zeros_like(row)), axis=1, keepdims=True)


def row_of(col):
    k = col.shape[0]
    eye = lax.broadcasted_iota(I32, (k, k), 0) == lax.broadcasted_iota(I32, (k, k), 1)
    return jnp.sum(jnp.where(eye, col, jnp.zeros_like(col)), axis=0, keepdims=True)


def tree_levels(codes):
    values = list(LEVELS)
    for bit in range(4):
        odd = (codes & (1 << bit)) != 0
        values = [jnp.where(odd, values[2 * i + 1], values[2 * i]) for i in range(len(values) // 2)]
    return values[0]


def dequant_kernel(first, codes_hbm, absmax_ref, *refs):
    weight_ref, token_ref, codes, sems = refs[-4:]
    chunks, block, cols = codes.shape
    blocks = absmax_ref.shape[1]
    per = cols // blocks

    def copy(i):
        rows = pl.ds(first + i * block, block)
        return pltpu.make_async_copy(codes_hbm.at[rows], codes.at[i], sems.at[i])

    for i in range(chunks):
        copy(i).start()
    token_ref[...] = jnp.zeros_like(token_ref)
    column_block = lax.broadcasted_iota(I32, (block, 128), 1) // per
    table = tree_levels(lax.broadcasted_iota(I32, (block, 128), 1) % 16)

    @pl.loop(0, chunks)
    def _(i):
        rows = pl.ds(pl.multiple_of(i * block, block), block)
        absmax = absmax_ref[pl.ds(pl.multiple_of(first + i * block, block), block), :]
        absmax = jnp.concatenate([absmax] * (128 // blocks), axis=1)
        copy(i).wait()
        for c in range(0, cols // 128, 2):
            values = []
            for tile in (c, c + 1):
                piece = codes[i, :, tile * 128 : (tile + 1) * 128]
                scale = jnp.take_along_axis(absmax, column_block + tile * (128 // per), axis=1, mode="promise_in_bounds")
                if tile % 4 == 1:
                    level = jnp.take_along_axis(table, piece, axis=1, mode="promise_in_bounds")
                else:
                    level = tree_levels(piece)
                values.append((level * scale).astype(BF))
            weight_ref[rows, c * 128 : (c + 2) * 128] = jnp.concatenate(values, axis=1)


def in_hbm(array):
    return pltpu.with_memory_space_constraint(array, pltpu.HBM)


def solution(mesh):
    n, tp = mesh.shape["seq"], mesh.shape["tp"]
    half = n // 2
    order = list(range(0, n, 2)) + list(range(n - 1, 0, -2))

    def ring(step):
        return [(order[i], order[(i + step) % n]) for i in range(n)]

    def flip(size, bit):
        return [(i, i ^ bit) for i in range(size)]

    def place(shard):
        return jnp.where(shard % 2 == 0, shard // 2, n - 1 - shard // 2)

    def shard_at(position):
        position = lax.rem(position + 2 * n, n)
        return jnp.where(position < half, 2 * position, 2 * (n - 1 - position) + 1)

    def body(
        residual,
        attention,
        quantized_codes,
        absmax,
        adapter_down,
        adapter_up,
        routed_slot_gate,
        selected,
        counts,
        cotangent,
    ):
        cap, all_heads = attention.shape
        tokens, cols = residual.shape
        heads = all_heads // n
        rank = adapter_up.shape[0]
        shares = 4 if tp % 4 == 0 and heads % 512 == 0 else 2
        sub = heads // shares
        wsub = heads // 2
        slots = n * cap
        side = 2 * rank
        down_t = adapter_down.T
        gate_row = routed_slot_gate.reshape(1, cap)
        selected_row = selected.reshape(1, cap)
        hbm = pl.BlockSpec(memory_space=pltpu.HBM)
        smem = pl.BlockSpec(memory_space=pltpu.SMEM)
        vmem = pl.BlockSpec(memory_space=pltpu.VMEM)

        def me():
            return lax.axis_index("seq"), lax.axis_index("tp") % 2

        def share():
            return lax.axis_index("tp") % shares

        def live_row(counts_ref):
            return lax.broadcasted_iota(I32, (1, cap), 1) < counts_ref[0]

        def pick(counts_ref, selected_ref):
            at = lax.broadcasted_iota(I32, (tokens, cap), 0) == selected_ref[...]
            return jnp.where(at & live_row(counts_ref), 1.0, 0.0).astype(BF)

        some = slots // 4
        live_slots = slots // 2

        def prepare(counts_ref, selected_ref, gate_ref, attention_ref, cot_ref, send_ref, own_ref, grad_ref, up_ref, chosen, gates, cots, sems):
            seq, _ = me()
            first = [
                pltpu.make_async_copy(selected_ref, chosen, sems.at[0]),
                pltpu.make_async_copy(gate_ref, gates, sems.at[1]),
                pltpu.make_async_copy(cot_ref, cots, sems.at[2]),
            ]
            later = []
            for k in range(half):
                for ref, flipped in ((send_ref, 1), (own_ref, 0)):
                    at = pl.multiple_of((seq ^ (2 * k + flipped)) * heads + share() * sub, 128)
                    sem = sems.at[3 + 2 * k + flipped]
                    later.append(pltpu.make_async_copy(attention_ref.at[:, pl.ds(at, sub)], ref.at[k], sem))
            for copy in first + later:
                copy.start()
            for copy in first:
                copy.wait()
            upstream = dot(pick(counts_ref, chosen), cots[...], 0, 0)
            up_ref[...] = upstream.astype(BF)
            live = column(jnp.where(live_row(counts_ref), 1.0, 0.0)) > 0
            grad_ref[...] = jnp.where(live, column(gates[...]) * upstream, DEAD).astype(BF)
            for copy in later:
                copy.wait()

        send, own, grad, upstream = call(
            prepare,
            [shape((half, cap, sub), BF)] * 2 + [shape((cap, cols), BF)] * 2,
            counts, in_hbm(selected_row), in_hbm(gate_row), in_hbm(attention), in_hbm(cotangent),
            in_specs=[smem] + [hbm] * 4,
            scratch=[
                pltpu.VMEM((1, cap), I32),
                pltpu.VMEM((1, cap), F32),
                pltpu.VMEM((tokens, cols), BF),
                pltpu.SemaphoreType.DMA((3 + n,)),
            ],
            name="prepare",
        )

        across = lax.ppermute(send, "seq", flip(n, 1))
        going, coming = lax.ppermute(grad, "seq", ring(1)), lax.ppermute(grad, "seq", ring(-1))
        block = min(64, wsub)

        def dequantize(part, *after):
            return call(
                functools.partial(dequant_kernel, part * wsub), [shape((wsub, cols), BF), shape((8, 128), F32)],
                in_hbm(quantized_codes), absmax, *after,
                in_specs=[hbm, vmem] + [vmem] * len(after), flops=wsub * cols * 100, name="dequantize",
                scratch=[
                    pltpu.VMEM((wsub // block, block, cols), I32),
                    pltpu.SemaphoreType.DMA((wsub // block,)),
                ],
            )

        weight0, mark = dequantize(0)
        across, going, coming, mark = lax.optimization_barrier((across, going, coming, mark))

        gathered = {0: (grad,)}

        def hop(step, going, coming):
            gathered[n - step], gathered[step] = (going,), (coming,)
            return lax.ppermute(going, "seq", ring(1)), lax.ppermute(coming, "seq", ring(-1))

        def pair(own_ref, across_ref, going_ref, coming_ref, token_ref, *refs):
            *refs, going_out_ref, coming_out_ref, token_out_ref = refs
            for k, ref in enumerate(refs):
                ref[0] = own_ref[k]
                ref[1] = across_ref[k]
            going_out_ref[...] = going_ref[...]
            coming_out_ref[...] = coming_ref[...]
            token_out_ref[...] = token_ref[...]

        def join(*refs):
            *refs, token_ref, out_ref = refs
            for k, ref in enumerate(refs):
                out_ref[2 * k * cap : 2 * (k + 1) * cap, :] = ref[...].reshape(2 * cap, sub)

        *pairs, going, coming, mark = call(
            pair, [shape((2, cap, sub), BF)] * half + [shape((cap, cols), BF)] * 2 + [shape((8, 128), F32)],
            own, across, going, coming, mark, name="pair",
        )
        fetched = [pairs[0]] + [lax.ppermute(pairs[k], "seq", flip(n, 2 * k)) for k in range(1, half)]
        going, coming = hop(1, going, coming)
        mid = cap // 2
        mid = cap // 2
        weight1, mark = dequantize(1, mark)
        weights = weight0, weight1
        fetched, going, coming, mark = lax.optimization_barrier((fetched, going, coming, mark))
        pieces = list(call(join, [shape((slots, sub), BF)], *fetched, mark, name="join"))
        for step in range(2, half - 1):
            going, coming = hop(step, going, coming)
        if shares == 4:
            pieces.append(lax.ppermute(pieces[0], "tp", flip(tp, 2)))
        pieces, going, coming = lax.optimization_barrier((pieces, going, coming))
        others = [lax.ppermute(piece, "tp", flip(tp, 1)) for piece in pieces]
        pieces = [pieces[0], others[0]] + ([pieces[1], others[1]] if shares == 4 else [])
        gathered[n - half + 1], gathered[half - 1] = (going,), (coming,)
        gathered[half] = (
            lax.ppermute(going[:mid], "seq", ring(1)),
            lax.ppermute(coming[mid:], "seq", ring(-1)),
        )

        def natural(refs):
            parts = [ref[...] for ref in refs]
            for bit in (1, 2)[: shares // 2]:
                unset = share() // bit % 2 == 0
                parts = [jnp.where(unset, parts[k], parts[k ^ bit]) for k in range(shares)]
            return jnp.concatenate(parts, axis=1)

        def forward(down_ref, up_ref, w0_ref, w1_ref, *refs):
            piece_refs, (out_ref, low_ref, every) = refs[:shares], refs[shares:]
            seq, _ = me()
            att = natural(piece_refs)
            low = dot(att, down_ref[...], 1, 1)
            thrice = jnp.concatenate(split3(adapter_scale * low), axis=1)
            for j in range(n):
                every[seq ^ j] = low[j * cap : (j + 1) * cap]
            top, bottom = every[:half].reshape(live_slots, rank), every[half:].reshape(live_slots, rank)
            low_ref[...] = jnp.concatenate([top, bottom], axis=1)
            spots = [lax.rem(place(seq ^ j) - place(seq) + n, n) for j in range(n)]
            tile = min(512, cols)
            for c in range(cols // tile):
                part = slice(c * tile, (c + 1) * tile)
                ups = up_ref[:, part]
                acc = dot(thrice, jnp.concatenate([ups] * 3, axis=0))
                acc = acc + dot(att[:, :wsub], w0_ref[:, part]) + dot(att[:, wsub:], w1_ref[:, part])
                acc = acc.astype(BF)
                for j in range(n):
                    out_ref[spots[j], :, part] = acc[j * cap : (j + 1) * cap]

        partial, low = call(
            forward,
            [shape((n, cap, cols), BF), shape((live_slots, side), F32)],
            down_t, adapter_up, *weights, *pieces,
            flops=2 * slots * heads * cols, name="forward", scratch=[pltpu.VMEM((n, cap, rank), F32)],
        )

        here, there = partial[half, :mid], partial[half, mid:]
        first_step = lax.ppermute(here, "seq", ring(1)), lax.ppermute(there, "seq", ring(-1))
        low_across = lax.ppermute(low, "seq", flip(n, 1))
        spots = [r for r in range(n) if r != half]

        def backward(up_ref, w0_ref, w1_ref, first_ref, second_ref, *refs):
            g_refs, (keep_ref, send_ref, live_ref, where_ref, every, sums) = refs[: n - 1], refs[n - 1 :]
            seq, core = me()
            for r, ref in zip(spots, g_refs):
                every[shard_at(place(seq) + r)] = ref[...]
            every[shard_at(place(seq) + half)] = jnp.concatenate([first_ref[...], second_ref[...]])
            passed = jnp.zeros((1, 1), F32)
            row = lax.broadcasted_iota(I32, (cap, live_slots), 0).astype(F32)
            col = lax.broadcasted_iota(I32, (cap, live_slots), 1).astype(F32)
            for j in range(n):
                alive = jnp.where(every[j][:, :1].astype(F32) < 0.5 * (1 + DEAD), 1.0, 0.0)
                at = jnp.where((row + passed == col) & (alive > 0), 1.0, 0.0)
                where_ref[j * cap : (j + 1) * cap, :] = at.astype(BF)
                passed = passed + jnp.sum(alive, axis=0, keepdims=True)
            g = dot(where_ref[...], every[...].reshape(slots, cols), 0, 0).astype(BF)
            live_ref[...] = g
            tile = min(256, wsub)
            for i in range(wsub // tile):
                for at, ref in ((0, w0_ref), (wsub, w1_ref)):
                    sums[:, at + i * tile : at + (i + 1) * tile] = dot(g, ref[i * tile : (i + 1) * tile, :], 1, 1)
            hi, lo = split2(adapter_scale * dot(g, up_ref[...], 1, 1))
            sums[:, heads:] = jnp.concatenate([hi, lo], axis=1).astype(F32)
            keep_ref[...] = sums[pl.ds(pl.multiple_of(core * some, 8), some), :]
            send_ref[...] = sums[pl.ds(pl.multiple_of((1 - core) * some, 8), some), :].astype(BF)

        def compact(low_ref, low_across_ref, where_ref, out_ref):
            low = low_ref[...] + low_across_ref[...]
            low = jnp.concatenate([low[:, :rank], low[:, rank:]], axis=0)
            low = dot(where_ref[...], jnp.concatenate(split3(low), axis=1), 0, 0)
            low = low[:, :rank] + low[:, rank : 2 * rank] + low[:, 2 * rank :]
            out_ref[...] = jnp.concatenate([low[: live_slots // 2], low[live_slots // 2 :]], axis=1)

        wide = heads + side

        def back(*farthest):
            return call(
                backward,
                [
                    shape((some, wide), F32),
                    shape((some, wide), BF),
                    shape((live_slots, cols), BF),
                    shape((slots, live_slots), BF),
                ],
                adapter_up, *weights, *farthest, *[gathered[r][0] for r in spots],
                flops=2 * live_slots * heads * cols,
                scratch=[pltpu.VMEM((n, cap, cols), BF), pltpu.VMEM((live_slots, wide), F32)],
                name="backward",
            )

        def ranks(a, b):
            return (a[:, heads : heads + rank].astype(F32) + b[:, heads : heads + rank].astype(F32)) + (
                a[:, heads + rank :].astype(F32) + b[:, heads + rank :].astype(F32)
            )

        def add(a_ref, b_ref, out_ref):
            a, b = a_ref[...], b_ref[...]
            out_ref[:, :heads] = (a[:, :heads].astype(F32) + b[:, :heads].astype(F32)).astype(BF)
            out_ref[:, heads:] = jnp.concatenate(split2(ranks(a, b)), axis=1)

        def finish(a_ref, b_ref, down_ref, low_ref, low_other_ref, out_ref, low_out_ref):
            low_out_ref[...] = low_ref[...] + low_other_ref[...]
            a, b = a_ref[...], b_ref[...]
            rank_grad = ranks(a, b).astype(BF)
            tail = dot(rank_grad, down_ref[...])
            out_ref[:, :heads] = (a[:, :heads].astype(F32) + b[:, :heads].astype(F32) + tail).astype(BF)
            out_ref[:, heads:] = jnp.concatenate([rank_grad, jnp.zeros_like(rank_grad)], axis=1)

        def plus(a, b):
            return (a.astype(F32) + b.astype(F32)).astype(BF)

        def sum_heads(keep, send):
            recv = yield lax.ppermute(send, "tp", flip(tp, 1))
            mine = call(add, [shape((some, wide), BF)], keep, recv, name="add")[0]
            bit = 2
            while 2 * bit < tp:
                recv = yield lax.ppermute(mine, "tp", flip(tp, bit))
                mine = call(add, [shape((some, wide), BF)], mine, recv, name="add")[0]
                bit *= 2
            recv = yield lax.ppermute(mine, "tp", flip(tp, bit))
            done, low_total = call(
                finish, [shape((some, wide), BF), shape((live_slots // 2, side), F32)],
                mine, recv, down_t, *low_terms, name="finish",
            )
            other_done = yield lax.ppermute(done, "tp", flip(tp, 1))
            return done, other_done, low_total

        def sum_low(total):
            bit = half // 2
            while bit > 1:
                recv = yield lax.ppermute(total, "seq", flip(n, bit))
                total = total + recv
                bit //= 2
            return total

        def drain(steps, value):
            try:
                while True:
                    value = steps.send(value)
            except StopIteration as stop:
                return stop.value

        going, coming = first_step
        for step in range(half - 1, 0, -1):
            here, there = partial[step], partial[n - step]
            if step == half - 1:
                here = jnp.concatenate([plus(here[:mid], going), here[mid:]])
                there = jnp.concatenate([there[:mid], plus(there[mid:], coming)])
                keep, send, grad_live, where_live = back(*gathered[half])
                here, there, send = lax.optimization_barrier((here, there, send))
            else:
                here, there = plus(here, going), plus(there, coming)
                if step == half - 2:
                    here, there, head_value, low_across = lax.optimization_barrier((here, there, head_value, low_across))
                else:
                    here, there = lax.optimization_barrier((here, there))
            going = lax.ppermute(here, "seq", ring(1))
            coming = lax.ppermute(there, "seq", ring(-1))
            if step == half - 1:
                head_steps, head_value = sum_heads(keep, send), None
            elif step == half - 2:
                low_live = call(compact, [shape((some, side), F32)], low, low_across, where_live, name="compact")[0]
                low_terms = low_live, lax.ppermute(low_live, "seq", flip(n, half))
            if step >= half - 2:
                head_value = head_steps.send(head_value)
        done, other_done, low_total = drain(head_steps, head_value)
        low_steps = sum_low(low_total)
        low_value = low_steps.send(None)
        def last(a_ref, b_ref, where_ref, *refs):
            piece_refs, (grad_ref, down_grad_ref, token_ref, live, rank_ref) = refs[:shares], refs[shares:]
            token_ref[...] = jnp.zeros_like(token_ref)
            seq, core = me()
            for ref, at in ((a_ref, core), (b_ref, 1 - core)):
                live[pl.ds(pl.multiple_of(at * some, 16), some), :] = ref[...]
            every = dot(where_ref[...], live[...]).astype(BF)
            grad_ref[...] = every[:, :heads]
            for j in range(n):
                rank_ref[j] = every[j * cap : (j + 1) * cap, heads:]
            rank_grad = jnp.concatenate([rank_ref[seq ^ j] for j in range(n)], axis=0)[:, :rank]
            for j, ref in enumerate(piece_refs):
                at = pl.multiple_of((share() ^ j) * sub, 128)
                down_grad_ref[:, pl.ds(at, sub)] = dot(rank_grad, ref[...], 0, 0)

        attention_output_grad, down_gradient, mark = call(
            last,
            [shape((slots, heads), BF), shape((rank, heads), F32), shape((8, 128), F32)],
            done, other_done, where_live, *pieces,
            scratch=[pltpu.VMEM((live_slots, wide), BF), pltpu.VMEM((n, cap, side), BF)], name="last",
        )

        going, coming, mark, low_value = lax.optimization_barrier((going, coming, mark, low_value))
        low_sum = drain(low_steps, low_value)

        def home(counts_ref, selected_ref, gate_ref, res_ref, own_ref, going_ref, coming_ref, up_ref, _, out_ref, gate_out_ref):
            chosen = pick(counts_ref, selected_ref)
            block = own_ref[...].astype(F32) + going_ref[...].astype(F32) + coming_ref[...].astype(F32)
            gate_out_ref[...] = row_of(jnp.sum(up_ref[...].astype(F32) * block, axis=1, keepdims=True))
            res = res_ref[...]
            picked = dot(chosen, res, 0, 0)
            updated = (picked + column(gate_ref[...]) * block).astype(BF)
            hit = jnp.sum(chosen.astype(F32), axis=1, keepdims=True) > 0
            out_ref[...] = jnp.where(hit, dot(chosen, updated), res.astype(F32)).astype(BF)

        outgoing_residual, gate_part = call(
            home,
            [shape((tokens, cols), BF), shape((1, cap), F32)],
            counts, selected_row, gate_row, residual, partial[0], going, coming, upstream, mark,
            in_specs=[smem] + [vmem] * 8, name="home",
        )
        bit = 1
        while bit < tp:
            gate_part = gate_part + lax.ppermute(gate_part, "tp", flip(tp, bit))
            bit *= 2

        def up_gradient(low_ref, g_ref, out_ref):
            low = jnp.concatenate([low_ref[:, :rank], low_ref[:, rank:]], axis=0)
            thrice = dot(jnp.concatenate(split3(low), axis=1), g_ref[...], 0, 0)
            out_ref[...] = adapter_scale * (
                thrice[:rank] + thrice[rank : 2 * rank] + thrice[2 * rank :]
            )

        adapter_up_gradient = call(
            up_gradient, [shape((rank, cols), F32)], low_sum, grad_live,
            flops=6 * live_slots * rank * cols, name="up_gradient",
        )[0]
        return (
            outgoing_residual,
            attention_output_grad,
            down_gradient.T,
            adapter_up_gradient,
            gate_part.reshape(cap),
        )

    return jax.shard_map(
        body,
        mesh=mesh,
        in_specs=(
            P("seq", "tp"),
            P("seq", None),
            P("seq", "tp"),
            P("seq", "tp"),
            P("seq", None),
            P(None, "tp"),
            P("seq"),
            P("seq"),
            P("seq"),
            P("seq", "tp"),
        ),
        out_specs=(P("seq", "tp"), P(None, "seq"), P("seq", None), P(None, "tp"), P("seq")),
        check_vma=False,
    )
```

```python
import functools

import jax
import jax.numpy as jnp
from jax import lax
from jax.experimental import pallas as pl
from jax.experimental.pallas import tpu as pltpu
from jax.sharding import PartitionSpec as P

LEVELS = (
    -1.0,
    -0.6961928009986877,
    -0.5250730514526367,
    -0.39491748809814453,
    -0.28444138169288635,
    -0.18477343022823334,
    -0.09105003625154495,
    0.0,
    0.07958029955625534,
    0.16093020141124725,
    0.24611230194568634,
    0.33791524171829224,
    0.44070982933044434,
    0.5626170039176941,
    0.7229568362236023,
    1.0,
)
adapter_scale = 0.25
BF, F32, I32 = jnp.bfloat16, jnp.float32, jnp.int32
VMEM_LIMIT = 16 * 2**20
DEAD = 2.0


def dot(a, b, ca=1, cb=0):
    return lax.dot_general(a, b, (((ca,), (cb,)), ((), ())), preferred_element_type=F32)


def split2(x):
    hi = x.astype(BF)
    return hi, (x - hi.astype(F32)).astype(BF)


def split3(x):
    hi = x.astype(BF)
    rest = x - hi.astype(F32)
    mid = rest.astype(BF)
    return hi, mid, (rest - mid.astype(F32)).astype(BF)


def call(kernel, outs, *args, flops=0, scratch=(), in_specs=None, name=None):
    nbytes = sum(a.size * a.dtype.itemsize for a in args) + sum(
        o.size * o.dtype.itemsize for o in outs
    )
    whole = pl.BlockSpec(memory_space=pltpu.VMEM)
    return pl.pallas_call(
        kernel,
        out_shape=tuple(outs),
        in_specs=in_specs or [whole] * len(args),
        out_specs=tuple([whole] * len(outs)),
        scratch_shapes=list(scratch),
        compiler_params=pltpu.CompilerParams(vmem_limit_bytes=VMEM_LIMIT),
        cost_estimate=pl.CostEstimate(flops=flops, bytes_accessed=nbytes, transcendentals=0),
        name=name,
    )(*args)


def shape(dims, dtype):
    return jax.ShapeDtypeStruct(tuple(dims), dtype)


def column(row):
    k = row.shape[1]
    eye = lax.broadcasted_iota(I32, (k, k), 0) == lax.broadcasted_iota(I32, (k, k), 1)
    return jnp.sum(jnp.where(eye, row, jnp.zeros_like(row)), axis=1, keepdims=True)


def row_of(col):
    k = col.shape[0]
    eye = lax.broadcasted_iota(I32, (k, k), 0) == lax.broadcasted_iota(I32, (k, k), 1)
    return jnp.sum(jnp.where(eye, col, jnp.zeros_like(col)), axis=0, keepdims=True)


def tree_levels(codes):
    values = list(LEVELS)
    for bit in range(4):
        odd = (codes & (1 << bit)) != 0
        values = [jnp.where(odd, values[2 * i + 1], values[2 * i]) for i in range(len(values) // 2)]
    return values[0]


def dequant_kernel(first, codes_hbm, absmax_ref, *refs):
    weight_ref, token_ref, codes, sems = refs[-4:]
    chunks, block, cols = codes.shape
    blocks = absmax_ref.shape[1]
    per = cols // blocks

    def copy(i):
        rows = pl.ds(first + i * block, block)
        return pltpu.make_async_copy(codes_hbm.at[rows], codes.at[i], sems.at[i])

    for i in range(chunks):
        copy(i).start()
    token_ref[...] = jnp.zeros_like(token_ref)
    column_block = lax.broadcasted_iota(I32, (block, 128), 1) // per
    table = tree_levels(lax.broadcasted_iota(I32, (block, 128), 1) % 16)

    @pl.loop(0, chunks)
    def _(i):
        rows = pl.ds(pl.multiple_of(i * block, block), block)
        absmax = absmax_ref[pl.ds(pl.multiple_of(first + i * block, block), block), :]
        absmax = jnp.concatenate([absmax] * (128 // blocks), axis=1)
        copy(i).wait()
        for c in range(0, cols // 128, 2):
            values = []
            for tile in (c, c + 1):
                piece = codes[i, :, tile * 128 : (tile + 1) * 128]
                scale = jnp.take_along_axis(absmax, column_block + tile * (128 // per), axis=1, mode="promise_in_bounds")
                if tile % 4 == 1:
                    level = jnp.take_along_axis(table, piece, axis=1, mode="promise_in_bounds")
                else:
                    level = tree_levels(piece)
                values.append((level * scale).astype(BF))
            weight_ref[rows, c * 128 : (c + 2) * 128] = jnp.concatenate(values, axis=1)


def in_hbm(array):
    return pltpu.with_memory_space_constraint(array, pltpu.HBM)


def solution(mesh):
    n, tp = mesh.shape["seq"], mesh.shape["tp"]
    half = n // 2
    order = list(range(0, n, 2)) + list(range(n - 1, 0, -2))

    def ring(step):
        return [(order[i], order[(i + step) % n]) for i in range(n)]

    def flip(size, bit):
        return [(i, i ^ bit) for i in range(size)]

    def place(shard):
        return jnp.where(shard % 2 == 0, shard // 2, n - 1 - shard // 2)

    def shard_at(position):
        position = lax.rem(position + 2 * n, n)
        return jnp.where(position < half, 2 * position, 2 * (n - 1 - position) + 1)

    def body(
        residual,
        attention,
        quantized_codes,
        absmax,
        adapter_down,
        adapter_up,
        routed_slot_gate,
        selected,
        counts,
        cotangent,
    ):
        cap, all_heads = attention.shape
        tokens, cols = residual.shape
        heads = all_heads // n
        rank = adapter_up.shape[0]
        shares = 4 if tp % 4 == 0 and heads % 512 == 0 else 2
        sub = heads // shares
        wsub = heads // 2
        slots = n * cap
        side = 2 * rank
        down_t = adapter_down.T
        gate_row = routed_slot_gate.reshape(1, cap)
        selected_row = selected.reshape(1, cap)
        hbm = pl.BlockSpec(memory_space=pltpu.HBM)
        smem = pl.BlockSpec(memory_space=pltpu.SMEM)
        vmem = pl.BlockSpec(memory_space=pltpu.VMEM)

        def me():
            return lax.axis_index("seq"), lax.axis_index("tp") % 2

        def share():
            return lax.axis_index("tp") % shares

        def live_row(counts_ref):
            return lax.broadcasted_iota(I32, (1, cap), 1) < counts_ref[0]

        def pick(counts_ref, selected_ref):
            at = lax.broadcasted_iota(I32, (tokens, cap), 0) == selected_ref[...]
            return jnp.where(at & live_row(counts_ref), 1.0, 0.0).astype(BF)

        some = slots // 4
        live_slots = slots // 2

        def prepare(counts_ref, selected_ref, gate_ref, attention_ref, cot_ref, send_ref, own_ref, grad_ref, up_ref, chosen, gates, cots, sems):
            seq, _ = me()
            first = [
                pltpu.make_async_copy(selected_ref, chosen, sems.at[0]),
                pltpu.make_async_copy(gate_ref, gates, sems.at[1]),
                pltpu.make_async_copy(cot_ref, cots, sems.at[2]),
            ]
            later = []
            for k in range(half):
                for ref, flipped in ((send_ref, 1), (own_ref, 0)):
                    at = pl.multiple_of((seq ^ (2 * k + flipped)) * heads + share() * sub, 128)
                    sem = sems.at[3 + 2 * k + flipped]
                    later.append(pltpu.make_async_copy(attention_ref.at[:, pl.ds(at, sub)], ref.at[k], sem))
            for copy in first + later:
                copy.start()
            for copy in first:
                copy.wait()
            upstream = dot(pick(counts_ref, chosen), cots[...], 0, 0)
            up_ref[...] = upstream.astype(BF)
            live = column(jnp.where(live_row(counts_ref), 1.0, 0.0)) > 0
            grad_ref[...] = jnp.where(live, column(gates[...]) * upstream, DEAD).astype(BF)
            for copy in later:
                copy.wait()

        send, own, grad, upstream = call(
            prepare,
            [shape((half, cap, sub), BF)] * 2 + [shape((cap, cols), BF)] * 2,
            counts, in_hbm(selected_row), in_hbm(gate_row), in_hbm(attention), in_hbm(cotangent),
            in_specs=[smem] + [hbm] * 4,
            scratch=[
                pltpu.VMEM((1, cap), I32),
                pltpu.VMEM((1, cap), F32),
                pltpu.VMEM((tokens, cols), BF),
                pltpu.SemaphoreType.DMA((3 + n,)),
            ],
            name="prepare",
        )

        across = lax.ppermute(send, "seq", flip(n, 1))
        going, coming = lax.ppermute(grad, "seq", ring(1)), lax.ppermute(grad, "seq", ring(-1))
        block = min(128, wsub)

        def dequantize(part, *after):
            return call(
                functools.partial(dequant_kernel, part * wsub), [shape((wsub, cols), BF), shape((8, 128), F32)],
                in_hbm(quantized_codes), absmax, *after,
                in_specs=[hbm, vmem] + [vmem] * len(after), flops=wsub * cols * 100, name="dequantize",
                scratch=[
                    pltpu.VMEM((wsub // block, block, cols), I32),
                    pltpu.SemaphoreType.DMA((wsub // block,)),
                ],
            )

        weight0, mark = dequantize(0)
        across, going, coming, mark = lax.optimization_barrier((across, going, coming, mark))

        gathered = {0: (grad,)}

        def hop(step, going, coming):
            gathered[n - step], gathered[step] = (going,), (coming,)
            return lax.ppermute(going, "seq", ring(1)), lax.ppermute(coming, "seq", ring(-1))

        def pair(own_ref, across_ref, going_ref, coming_ref, token_ref, *refs):
            *refs, going_out_ref, coming_out_ref, token_out_ref = refs
            for k, ref in enumerate(refs):
                ref[0] = own_ref[k]
                ref[1] = across_ref[k]
            going_out_ref[...] = going_ref[...]
            coming_out_ref[...] = coming_ref[...]
            token_out_ref[...] = token_ref[...]

        def join(*refs):
            *refs, token_ref, out_ref = refs
            for k, ref in enumerate(refs):
                out_ref[2 * k * cap : 2 * (k + 1) * cap, :] = ref[...].reshape(2 * cap, sub)

        *pairs, going, coming, mark = call(
            pair, [shape((2, cap, sub), BF)] * half + [shape((cap, cols), BF)] * 2 + [shape((8, 128), F32)],
            own, across, going, coming, mark, name="pair",
        )
        fetched = [pairs[0]] + [lax.ppermute(pairs[k], "seq", flip(n, 2 * k)) for k in range(1, half)]
        going, coming = hop(1, going, coming)
        mid = cap // 2
        mid = cap // 2
        weight1, mark = dequantize(1, mark)
        weights = weight0, weight1
        fetched, going, coming, mark = lax.optimization_barrier((fetched, going, coming, mark))
        pieces = list(call(join, [shape((slots, sub), BF)], *fetched, mark, name="join"))
        for step in range(2, half - 1):
            going, coming = hop(step, going, coming)
        if shares == 4:
            pieces.append(lax.ppermute(pieces[0], "tp", flip(tp, 2)))
        pieces, going, coming = lax.optimization_barrier((pieces, going, coming))
        others = [lax.ppermute(piece, "tp", flip(tp, 1)) for piece in pieces]
        pieces = [pieces[0], others[0]] + ([pieces[1], others[1]] if shares == 4 else [])
        gathered[n - half + 1], gathered[half - 1] = (going,), (coming,)
        gathered[half] = (
            lax.ppermute(going[:mid], "seq", ring(1)),
            lax.ppermute(coming[mid:], "seq", ring(-1)),
        )

        def natural(refs):
            parts = [ref[...] for ref in refs]
            for bit in (1, 2)[: shares // 2]:
                unset = share() // bit % 2 == 0
                parts = [jnp.where(unset, parts[k], parts[k ^ bit]) for k in range(shares)]
            return jnp.concatenate(parts, axis=1)

        def forward(down_ref, up_ref, w0_ref, w1_ref, *refs):
            piece_refs, (out_ref, low_ref, every) = refs[:shares], refs[shares:]
            seq, _ = me()
            att = natural(piece_refs)
            low = dot(att, down_ref[...], 1, 1)
            thrice = jnp.concatenate(split3(adapter_scale * low), axis=1)
            for j in range(n):
                every[seq ^ j] = low[j * cap : (j + 1) * cap]
            top, bottom = every[:half].reshape(live_slots, rank), every[half:].reshape(live_slots, rank)
            low_ref[...] = jnp.concatenate([top, bottom], axis=1)
            spots = [lax.rem(place(seq ^ j) - place(seq) + n, n) for j in range(n)]
            tile = min(512, cols)
            for c in range(cols // tile):
                part = slice(c * tile, (c + 1) * tile)
                ups = up_ref[:, part]
                acc = dot(thrice, jnp.concatenate([ups] * 3, axis=0))
                acc = acc + dot(att[:, :wsub], w0_ref[:, part]) + dot(att[:, wsub:], w1_ref[:, part])
                acc = acc.astype(BF)
                for j in range(n):
                    out_ref[spots[j], :, part] = acc[j * cap : (j + 1) * cap]

        partial, low = call(
            forward,
            [shape((n, cap, cols), BF), shape((live_slots, side), F32)],
            down_t, adapter_up, *weights, *pieces,
            flops=2 * slots * heads * cols, name="forward", scratch=[pltpu.VMEM((n, cap, rank), F32)],
        )

        here, there = partial[half, :mid], partial[half, mid:]
        first_step = lax.ppermute(here, "seq", ring(1)), lax.ppermute(there, "seq", ring(-1))
        low_across = lax.ppermute(low, "seq", flip(n, 1))
        spots = [r for r in range(n) if r != half]

        def backward(up_ref, w0_ref, w1_ref, first_ref, second_ref, *refs):
            g_refs, (keep_ref, send_ref, live_ref, where_ref, every, sums) = refs[: n - 1], refs[n - 1 :]
            seq, core = me()
            for r, ref in zip(spots, g_refs):
                every[shard_at(place(seq) + r)] = ref[...]
            every[shard_at(place(seq) + half)] = jnp.concatenate([first_ref[...], second_ref[...]])
            passed = jnp.zeros((1, 1), F32)
            row = lax.broadcasted_iota(I32, (cap, live_slots), 0).astype(F32)
            col = lax.broadcasted_iota(I32, (cap, live_slots), 1).astype(F32)
            for j in range(n):
                alive = jnp.where(every[j][:, :1].astype(F32) < 0.5 * (1 + DEAD), 1.0, 0.0)
                at = jnp.where((row + passed == col) & (alive > 0), 1.0, 0.0)
                where_ref[j * cap : (j + 1) * cap, :] = at.astype(BF)
                passed = passed + jnp.sum(alive, axis=0, keepdims=True)
            g = dot(where_ref[...], every[...].reshape(slots, cols), 0, 0).astype(BF)
            live_ref[...] = g
            tile = min(256, wsub)
            for i in range(wsub // tile):
                for at, ref in ((0, w0_ref), (wsub, w1_ref)):
                    sums[:, at + i * tile : at + (i + 1) * tile] = dot(g, ref[i * tile : (i + 1) * tile, :], 1, 1)
            hi, lo = split2(adapter_scale * dot(g, up_ref[...], 1, 1))
            sums[:, heads:] = jnp.concatenate([hi, lo], axis=1).astype(F32)
            keep_ref[...] = sums[pl.ds(pl.multiple_of(core * some, 8), some), :]
            send_ref[...] = sums[pl.ds(pl.multiple_of((1 - core) * some, 8), some), :].astype(BF)

        def compact(low_ref, low_across_ref, where_ref, out_ref):
            low = low_ref[...] + low_across_ref[...]
            low = jnp.concatenate([low[:, :rank], low[:, rank:]], axis=0)
            low = dot(where_ref[...], jnp.concatenate(split3(low), axis=1), 0, 0)
            low = low[:, :rank] + low[:, rank : 2 * rank] + low[:, 2 * rank :]
            out_ref[...] = jnp.concatenate([low[: live_slots // 2], low[live_slots // 2 :]], axis=1)

        wide = heads + side

        def back(*farthest):
            return call(
                backward,
                [
                    shape((some, wide), F32),
                    shape((some, wide), BF),
                    shape((live_slots, cols), BF),
                    shape((slots, live_slots), BF),
                ],
                adapter_up, *weights, *farthest, *[gathered[r][0] for r in spots],
                flops=2 * live_slots * heads * cols,
                scratch=[pltpu.VMEM((n, cap, cols), BF), pltpu.VMEM((live_slots, wide), F32)],
                name="backward",
            )

        def ranks(a, b):
            return (a[:, heads : heads + rank].astype(F32) + b[:, heads : heads + rank].astype(F32)) + (
                a[:, heads + rank :].astype(F32) + b[:, heads + rank :].astype(F32)
            )

        def add(a_ref, b_ref, out_ref):
            a, b = a_ref[...], b_ref[...]
            out_ref[:, :heads] = (a[:, :heads].astype(F32) + b[:, :heads].astype(F32)).astype(BF)
            out_ref[:, heads:] = jnp.concatenate(split2(ranks(a, b)), axis=1)

        def finish(a_ref, b_ref, down_ref, low_ref, low_other_ref, out_ref, low_out_ref):
            low_out_ref[...] = low_ref[...] + low_other_ref[...]
            a, b = a_ref[...], b_ref[...]
            rank_grad = ranks(a, b).astype(BF)
            tail = dot(rank_grad, down_ref[...])
            out_ref[:, :heads] = (a[:, :heads].astype(F32) + b[:, :heads].astype(F32) + tail).astype(BF)
            out_ref[:, heads:] = jnp.concatenate([rank_grad, jnp.zeros_like(rank_grad)], axis=1)

        def plus(a, b):
            return (a.astype(F32) + b.astype(F32)).astype(BF)

        def sum_heads(keep, send):
            recv = yield lax.ppermute(send, "tp", flip(tp, 1))
            mine = call(add, [shape((some, wide), BF)], keep, recv, name="add")[0]
            bit = 2
            while 2 * bit < tp:
                recv = yield lax.ppermute(mine, "tp", flip(tp, bit))
                mine = call(add, [shape((some, wide), BF)], mine, recv, name="add")[0]
                bit *= 2
            recv = yield lax.ppermute(mine, "tp", flip(tp, bit))
            done, low_total = call(
                finish, [shape((some, wide), BF), shape((live_slots // 2, side), F32)],
                mine, recv, down_t, *low_terms, name="finish",
            )
            other_done = yield lax.ppermute(done, "tp", flip(tp, 1))
            return done, other_done, low_total

        def sum_low(total):
            bit = half // 2
            while bit > 1:
                recv = yield lax.ppermute(total, "seq", flip(n, bit))
                total = total + recv
                bit //= 2
            return total

        def drain(steps, value):
            try:
                while True:
                    value = steps.send(value)
            except StopIteration as stop:
                return stop.value

        going, coming = first_step
        for step in range(half - 1, 0, -1):
            here, there = partial[step], partial[n - step]
            if step == half - 1:
                here = jnp.concatenate([plus(here[:mid], going), here[mid:]])
                there = jnp.concatenate([there[:mid], plus(there[mid:], coming)])
                keep, send, grad_live, where_live = back(*gathered[half])
                here, there, send = lax.optimization_barrier((here, there, send))
            else:
                here, there = plus(here, going), plus(there, coming)
                if step == half - 2:
                    here, there, head_value, low_across = lax.optimization_barrier((here, there, head_value, low_across))
                else:
                    here, there = lax.optimization_barrier((here, there))
            going = lax.ppermute(here, "seq", ring(1))
            coming = lax.ppermute(there, "seq", ring(-1))
            if step == half - 1:
                head_steps, head_value = sum_heads(keep, send), None
            elif step == half - 2:
                low_live = call(compact, [shape((some, side), F32)], low, low_across, where_live, name="compact")[0]
                low_terms = low_live, lax.ppermute(low_live, "seq", flip(n, half))
            if step >= half - 2:
                head_value = head_steps.send(head_value)
        done, other_done, low_total = drain(head_steps, head_value)
        low_steps = sum_low(low_total)
        low_value = low_steps.send(None)
        def last(a_ref, b_ref, where_ref, *refs):
            piece_refs, (grad_ref, down_grad_ref, token_ref, live, rank_ref) = refs[:shares], refs[shares:]
            token_ref[...] = jnp.zeros_like(token_ref)
            seq, core = me()
            for ref, at in ((a_ref, core), (b_ref, 1 - core)):
                live[pl.ds(pl.multiple_of(at * some, 16), some), :] = ref[...]
            every = dot(where_ref[...], live[...]).astype(BF)
            grad_ref[...] = every[:, :heads]
            for j in range(n):
                rank_ref[j] = every[j * cap : (j + 1) * cap, heads:]
            rank_grad = jnp.concatenate([rank_ref[seq ^ j] for j in range(n)], axis=0)[:, :rank]
            for j, ref in enumerate(piece_refs):
                at = pl.multiple_of((share() ^ j) * sub, 128)
                down_grad_ref[:, pl.ds(at, sub)] = dot(rank_grad, ref[...], 0, 0)

        attention_output_grad, down_gradient, mark = call(
            last,
            [shape((slots, heads), BF), shape((rank, heads), F32), shape((8, 128), F32)],
            done, other_done, where_live, *pieces,
            scratch=[pltpu.VMEM((live_slots, wide), BF), pltpu.VMEM((n, cap, side), BF)], name="last",
        )

        going, coming, mark, low_value = lax.optimization_barrier((going, coming, mark, low_value))
        low_sum = drain(low_steps, low_value)

        def home(counts_ref, selected_ref, gate_ref, res_ref, own_ref, going_ref, coming_ref, up_ref, _, out_ref, gate_out_ref):
            chosen = pick(counts_ref, selected_ref)
            block = own_ref[...].astype(F32) + going_ref[...].astype(F32) + coming_ref[...].astype(F32)
            gate_out_ref[...] = row_of(jnp.sum(up_ref[...].astype(F32) * block, axis=1, keepdims=True))
            res = res_ref[...]
            picked = dot(chosen, res, 0, 0)
            updated = (picked + column(gate_ref[...]) * block).astype(BF)
            hit = jnp.sum(chosen.astype(F32), axis=1, keepdims=True) > 0
            out_ref[...] = jnp.where(hit, dot(chosen, updated), res.astype(F32)).astype(BF)

        outgoing_residual, gate_part = call(
            home,
            [shape((tokens, cols), BF), shape((1, cap), F32)],
            counts, selected_row, gate_row, residual, partial[0], going, coming, upstream, mark,
            in_specs=[smem] + [vmem] * 8, name="home",
        )
        bit = 1
        while bit < tp:
            gate_part = gate_part + lax.ppermute(gate_part, "tp", flip(tp, bit))
            bit *= 2

        def up_gradient(low_ref, g_ref, out_ref):
            low = jnp.concatenate([low_ref[:, :rank], low_ref[:, rank:]], axis=0)
            thrice = dot(jnp.concatenate(split3(low), axis=1), g_ref[...], 0, 0)
            out_ref[...] = adapter_scale * (
                thrice[:rank] + thrice[rank : 2 * rank] + thrice[2 * rank :]
            )

        adapter_up_gradient = call(
            up_gradient, [shape((rank, cols), F32)], low_sum, grad_live,
            flops=6 * live_slots * rank * cols, name="up_gradient",
        )[0]
        return (
            outgoing_residual,
            attention_output_grad,
            down_gradient.T,
            adapter_up_gradient,
            gate_part.reshape(cap),
        )

    return jax.shard_map(
        body,
        mesh=mesh,
        in_specs=(
            P("seq", "tp"),
            P("seq", None),
            P("seq", "tp"),
            P("seq", "tp"),
            P("seq", None),
            P(None, "tp"),
            P("seq"),
            P("seq"),
            P("seq"),
            P("seq", "tp"),
        ),
        out_specs=(P("seq", "tp"), P(None, "seq"), P("seq", None), P(None, "tp"), P("seq")),
        check_vma=False,
    )
```
